256 devices in a mesh: grp: 16 (over x, y_lo, core), tp: 16 (over z, y_hi).
Axes of the slice: x: 4, y: 4 (y_hi: 2, y_lo: 2; y = y_hi * 2 + y_lo), z: 8, core: 2. Of those that a mesh axis runs over, the one named last changes fastest.
Arguments:
- hidden: bfloat16 [2, 32768, 8192], P(None, ('grp', 'tp')), may hold values from -6 to 6
- norm_gain: float32 [8192], replicated, may hold values from 0.1 to 1.9
- kv_weight: bfloat16 [8192, 1024], P(('grp', 'tp')), may hold values from -0.0625 to 0.0625
- queries: bfloat16 [2, 32768, 4096], P(None, 'grp', 'tp'), may hold values from -512 to 512
- positions: int32 [32768], P(('grp', 'tp')), may hold values from 0 to 2047, as said below
Outputs:
- attended: bfloat16 [2, 32768, 4096], P(None, ('grp', 'tp'))
The draws below stay inside these ranges and needn't reach their ends.
Inputs may be any that keep to these rules, and one draw needn't show every extreme that they name: Inside each sequence of 2048 tokens positions count up by one and restart at 0 where a document begins; every sequence begins with 0, and the first sequence is one document.
All inputs are finite; a program needn't handle non-finite values.
Results may differ from the reference program's by a relative error of at most 0.011.
The reference program's roundings to bfloat16 on the way (of `normed` and `rotated`) count: a program that leaves them out, or rounds other values in their place, can miss the bound.
Values may be sent and summed in bfloat16 or wider, within the bound.
No kernel may reach another device: no remote copies, remote signals or barrier semaphores. Data moves between devices by JAX's collectives and lax.ppermute only.
A program may use at most 192 MiB of HBM per device.

```python
import math
import jax
import jax.numpy as jnp
from jax import lax

D = 8192
HD = 128
QH = 32
KVH = 4
STEPS = 2
TOK_DEV = 128
SEQ = 2048
TOKENS = 32768
N_GRP = 16


def draw_positions(key, part):
    key = jax.random.fold_in(key, 11)
    starts = jax.random.randint(key, (N_GRP, SEQ), 0, 3 * TOK_DEV) == 0
    starts = starts.at[:, 0].set(True)
    starts = starts.at[0, 1:].set(False)
    counter = jnp.broadcast_to(jnp.arange(SEQ, dtype=jnp.int32), (N_GRP, SEQ))
    latest = lax.cummax(jnp.where(starts, counter, 0), axis=1)
    return (counter - latest).reshape(N_GRP * SEQ).astype(jnp.int32)


def draw_queries(key, part):
    key = jax.random.fold_in(key, 23)
    base_key = jax.random.fold_in(key, 1)
    level_key = jax.random.fold_in(key, 2)
    base = jnp.clip(jax.random.normal(base_key, (STEPS, TOKENS, QH, HD), jnp.float32), -4.0, 4.0)
    level = jnp.exp(jax.random.uniform(level_key, (STEPS, TOKENS, QH, 1), jnp.float32, 0.0, math.log(128.0)))
    return (base * level).reshape(STEPS, TOKENS, QH * HD).astype(jnp.bfloat16)


def shard_levels(stream_key, extent, split, smallest, top_value):
    level, own = 1.0, jax.random.fold_in(stream_key, 6)
    for axis_at, parts in split:
        steps = jnp.exp(jax.random.uniform(jax.random.fold_in(own, axis_at), (parts,), jnp.float32, smallest / len(split), top_value / len(split)))
        level = level * jnp.repeat(steps, extent[axis_at] // parts).reshape([-1 if axis == axis_at else 1 for axis in range(len(extent))])
    return level


def normal_values(key, dims, spread, reach, shards=(), held_as=jnp.bfloat16):
    level = shard_levels(key, dims, shards, -0.22, 0.18) if shards else 1.0
    drawn = jax.random.normal(key, dims, jnp.float32) * spread * level
    return jnp.minimum(jnp.maximum(drawn, -reach), reach).astype(held_as)


def setup_inputs(seed: int = 0) -> dict:
    arg_keys = jax.random.split(jax.random.key(seed), 6)
    hidden = normal_values(arg_keys[0], (STEPS, TOKENS, D), 1.0, 6.0, ((1, 256),))
    norm_gain = jnp.clip(1.0 + 0.18 * jax.random.normal(arg_keys[1], (D,), jnp.float32), 0.1, 1.9)
    kv_weight = normal_values(arg_keys[2], (D, 2 * KVH * HD), D ** -0.5, 0.0625, ((0, 256),))
    queries = draw_queries(jax.random.fold_in(arg_keys[5], 71), 0)
    positions = draw_positions(jax.random.fold_in(arg_keys[5], 71), 0)
    return dict(hidden=hidden, norm_gain=norm_gain, kv_weight=kv_weight, queries=queries, positions=positions)


rope_base = 500000.0

def rotate(values, positions):
    half = values.shape[-1] // 2
    freqs = rope_base ** (-jnp.arange(half, dtype=jnp.float32) * 2.0 / values.shape[-1])
    angles = positions.astype(jnp.float32)[:, None] * freqs[None, :]
    cosine = jnp.cos(angles)[:, None, :]
    sine = jnp.sin(angles)[:, None, :]
    first = values[..., :half]
    second = values[..., half:]
    return jnp.concatenate([first * cosine - second * sine, second * cosine + first * sine], axis=-1)

def keys_values(hidden, norm_gain, kv_weight):
    wide = hidden.astype(jnp.float32)
    scale = lax.rsqrt(lax.optimization_barrier(jnp.mean(wide * wide, axis=-1, keepdims=True)) + 1e-05)
    normed = (wide * scale * norm_gain.astype(jnp.float32)).astype(jnp.bfloat16)
    return jnp.dot(normed, kv_weight, preferred_element_type=jnp.float32)

def reference(hidden, norm_gain, kv_weight, queries, positions):
    pair_cols = kv_weight.shape[1]
    half = pair_cols // 2
    heads_kv = half // HD
    groups = QH // heads_kv
    block = min(512, SEQ)
    inv_root = 1.0 / math.sqrt(HD)

    def replica(number):
        begin = (number * SEQ).astype(jnp.int32)
        hid = lax.dynamic_slice_in_dim(hidden, begin, SEQ, 1)
        query_part = lax.dynamic_slice_in_dim(queries, begin, SEQ, 1)
        place = lax.dynamic_slice_in_dim(positions, begin, SEQ, 0)
        projected = keys_values(hid.reshape(STEPS * SEQ, D), norm_gain, kv_weight).reshape(STEPS, SEQ, pair_cols)
        keys = jnp.stack([rotate(projected[other, :, :half].reshape(SEQ, heads_kv, HD), place) for other in range(STEPS)]).astype(jnp.bfloat16)
        values = projected[..., half:].reshape(STEPS, SEQ, heads_kv, HD).astype(jnp.bfloat16)
        rotated = jnp.stack([rotate(query_part[other].reshape(SEQ, QH, HD), place) for other in range(STEPS)]).astype(jnp.bfloat16)
        rotated = rotated.reshape(STEPS, SEQ, heads_kv, groups, HD)

        def one_block(bnumber):
            start = (bnumber * block).astype(jnp.int32)
            query_block = lax.dynamic_slice_in_dim(rotated, start, block, 1).astype(jnp.float32)
            place_block = lax.dynamic_slice_in_dim(place, start, block, 0)
            query_index = start + jnp.arange(block, dtype=jnp.int32)
            key_index = jnp.arange(SEQ, dtype=jnp.int32)
            allowed = (key_index[None, :] <= query_index[:, None]) & (query_index[:, None] - key_index[None, :] <= place_block[:, None])
            scores = jnp.einsum('sqhgd,khd->sqhgk', query_block, keys[0].astype(jnp.float32)) * inv_root
            scores = jnp.where(allowed[None, :, None, None, :], scores, -1e+30)
            results = []
            for step in range(STEPS):
                diagonal = []
                for other in range(1, step + 1):
                    own_keys = lax.dynamic_slice_in_dim(keys[other], start, block, 0).astype(jnp.float32)
                    diagonal.append(lax.optimization_barrier(jnp.sum(query_block[step] * own_keys[:, :, None, :], axis=-1)) * inv_root)
                best = scores[step].max(-1)
                for score in diagonal:
                    best = jnp.maximum(best, score)
                weights = jnp.where(allowed[:, None, None, :], jnp.exp(scores[step] - best[..., None]), 0.0)
                total = weights.sum(-1)
                rounded = lax.optimization_barrier(weights.astype(jnp.bfloat16)).astype(jnp.float32)
                accum = jnp.einsum('qhgk,khd->qhgd', rounded, values[0].astype(jnp.float32))
                for offset, score in enumerate(diagonal):
                    weight = jnp.exp(score - best)
                    total = total + weight
                    own_values = lax.dynamic_slice_in_dim(values[offset + 1], start, block, 0).astype(jnp.float32)
                    weight_round = lax.optimization_barrier(weight.astype(jnp.bfloat16)).astype(jnp.float32)
                    accum = accum + weight_round[..., None] * own_values[:, :, None, :]
                results.append((accum / total[..., None]).astype(jnp.bfloat16).reshape(block, QH * HD))
            return jnp.stack(results)
        blocks = lax.map(one_block, jnp.arange(SEQ // block, dtype=jnp.int32))
        return blocks.transpose(1, 0, 2, 3).reshape(STEPS, SEQ, QH * HD)
    result = lax.map(replica, jnp.arange(N_GRP, dtype=jnp.int32))
    return result.transpose(1, 0, 2, 3).reshape(STEPS, TOKENS, QH * HD)
```

```python
import math

import jax
import jax.numpy as jnp
from jax import lax
from jax.experimental import pallas as pl
from jax.experimental.pallas import tpu as pltpu
from jax.sharding import PartitionSpec as P

HD = 128
QH = 32
KVH = 4
BOTH = ("grp", "tp")
COLS_A = 640
SLOTS_Z = (0, -1, 1, -2, 2, -3, 3, -4)
SLOTS_4 = (0, -1, 1, -2)
BLOCK = 512
TILE = 512
VMEM = 56 * 1024 * 1024
NEG = -1e30
rope_base = 500000.0


def coords(grp, tp):
    return grp // 4, (tp % 2) * 2 + (grp // 2) % 2, tp // 2, grp % 2


def place(x, y, z, core):
    return ((x * 2 + y % 2) * 2 + core) * 16 + z * 2 + y // 2


def shift(value, dx=0, dy=0, dz=0, swap=False):
    pairs = []
    for device in range(256):
        x, y, z, core = coords(device // 16, device % 16)
        target = place((x + dx) % 4, (y + dy) % 4, (z + dz) % 8, 1 - core if swap else core)
        pairs.append((device, target))
    return lax.ppermute(value, BOTH, pairs)


def ring8(block):
    up, down = shift(block, dz=1), shift(block, dz=-1)
    found = [block, up, down]
    for _ in range(2):
        up, down = shift(up, dz=1), shift(down, dz=-1)
        found += [up, down]
    found.append(shift(up, dz=1))
    return found


def ring4(block, axis):
    half = block.shape[0] // 2
    up, down = shift(block, **{axis: 1}), shift(block, **{axis: -1})
    far = shift(up[:half], **{axis: 1}), shift(down[half:], **{axis: -1})
    return [block, up, down, far[0], far[1]]


def norm_body(core_ref, hidden_ref, gain_ref, mine_ref, other_ref):
    core = core_ref[0]
    wide = hidden_ref[...].astype(jnp.float32)
    scale = lax.rsqrt(jnp.mean(wide * wide, axis=-1, keepdims=True) + 1e-05)
    for group in range(8):
        for out_ref, which in ((mine_ref, core), (other_ref, 1 - core)):
            start = pl.multiple_of((2 * group + which) * 512, 512)
            part = hidden_ref[:, pl.ds(start, 512)].astype(jnp.float32)
            gain = gain_ref[:, pl.ds(start, 512)]
            out_ref[:, group * 512 : (group + 1) * 512] = (part * scale * gain).astype(jnp.bfloat16)


def norm(hidden, gain, core):
    rows, width = hidden.shape
    out = jax.ShapeDtypeStruct((rows, width // 2), jnp.bfloat16)
    return pl.pallas_call(
        norm_body,
        out_shape=(out, out),
        grid=(rows // 64,),
        in_specs=[
            pl.BlockSpec(memory_space=pltpu.SMEM),
            pl.BlockSpec((64, width), lambda i: (i, 0)),
            pl.BlockSpec((1, width), lambda i: (0, 0)),
        ],
        out_specs=(
            pl.BlockSpec((64, width // 2), lambda i: (i, 0)),
            pl.BlockSpec((64, width // 2), lambda i: (i, 0)),
        ),
        compiler_params=pltpu.CompilerParams(vmem_limit_bytes=VMEM),
        name="norm",
    )(core, hidden, gain)


def project_body(where_ref, mine_ref, other_ref, *refs):
    a_refs, b_refs = refs[0:5], refs[5:10]
    out_ref, weight = refs[10], refs[11]
    x0, y0, z0 = where_ref[0], where_ref[1], where_ref[2]
    last = ((0, 0, 4), (-1, 0, 4), (1, 0, 4), (-2, 0, 2), (-2, 2, 2))

    def rel(slot):
        step = (slot + 1) // 2
        return jnp.where(slot % 2 == 1, -step, step)

    for which, group in ((0, a_refs), (1, b_refs)):
        for ref, (off, first, count) in zip(group, last):
            lo, hi = (0, COLS_A) if which == 0 else (COLS_A, weight.shape[1])

            def copy(index, _, ref=ref, off=off, first=first, which=which, lo=lo, hi=hi):
                mid, zslot = index // 8, index % 8
                other = rel(mid + first)
                x = (x0 + (off if which == 0 else other) + 4) % 4
                y = (y0 + (other if which == 0 else off) + 4) % 4
                z = (z0 + rel(zslot) + 8) % 8
                row = (x * 2 + y % 2) * 512 + z * 64 + (y // 2) * 32
                weight[pl.ds(pl.multiple_of(row, 32), 32), lo:hi] = ref[mid, zslot]
                return 0

            lax.fori_loop(0, count * 8, copy, 0)
    rows = mine_ref.shape[0]
    for index, ref in enumerate((mine_ref, other_ref)):
        out_ref[index * rows : (index + 1) * rows, :] = jnp.dot(
            ref[...], weight[...], preferred_element_type=jnp.float32
        )


def project(where, mine, other, pieces_a, pieces_b):
    rows, depth = mine.shape
    cols = pieces_a[0].shape[-1] + pieces_b[0].shape[-1]
    vmem = pl.BlockSpec(memory_space=pltpu.VMEM)
    return pl.pallas_call(
        project_body,
        out_shape=jax.ShapeDtypeStruct((2 * rows, cols), jnp.float32),
        in_specs=[pl.BlockSpec(memory_space=pltpu.SMEM)] + [vmem] * 12,
        out_specs=vmem,
        scratch_shapes=[pltpu.VMEM((depth, cols), jnp.bfloat16)],
        compiler_params=pltpu.CompilerParams(vmem_limit_bytes=VMEM),
        name="project",
    )(where, mine, other, *pieces_a, *pieces_b)


def turn(values, cosine, sine):
    return values * cosine + pltpu.roll(values, 64, 1) * sine


def keys_values_body(own_ref, got_ref, cos_ref, sin_ref, first_ref, second_ref):
    rows = first_ref.shape[0]
    cosine, sine = cos_ref[...], sin_ref[...]
    for step, out_ref in enumerate((first_ref, second_ref)):
        for head in range(2 * KVH):
            cols = slice(head * HD, (head + 1) * HD)
            part = own_ref[step * rows : (step + 1) * rows, cols]
            part = part + got_ref[step * rows : (step + 1) * rows, cols]
            if head < KVH:
                part = turn(part, cosine, sine)
            out_ref[:, cols] = part.astype(jnp.bfloat16)


def keys_values(own, got, cosine, sine):
    rows, cols = own.shape
    out = jax.ShapeDtypeStruct((rows // 2, cols), jnp.bfloat16)
    vmem = pl.BlockSpec(memory_space=pltpu.VMEM)
    return pl.pallas_call(
        keys_values_body,
        out_shape=(out, out),
        in_specs=[vmem] * 4,
        out_specs=(vmem, vmem),
        compiler_params=pltpu.CompilerParams(vmem_limit_bytes=VMEM),
        name="keys_values",
    )(own, got, cosine, sine)


def attend_body(info_ref, q_ref, cos_ref, sin_ref, low_ref, k1_ref, v1_ref, *refs):
    k_refs, v_refs = refs[0:8], refs[8:16]
    out_ref, keys, values, scores, maxima, rotated = refs[16:]
    z0, first, low_first, low_last = info_ref[0], info_ref[1], info_ref[2], info_ref[3]
    rows = low_ref.shape[0]
    inv_root = 1.0 / math.sqrt(HD)
    to_two = inv_root * math.log2(math.e)

    for off, k_ref, v_ref in zip(SLOTS_Z, k_refs, v_refs):
        start = pl.multiple_of(((z0 + off + 8) % 8) * 256, 256)
        keys[pl.ds(start, 256), :] = k_ref[...]
        values[pl.ds(start, 256), :HD] = v_ref[...]
    values[:, HD:] = jnp.ones((values.shape[0], HD), jnp.bfloat16)

    cosine, sine = cos_ref[...], sin_ref[...]
    begin = low_first // BLOCK
    end = (first + rows - 1) // BLOCK + 1
    token = first + lax.broadcasted_iota(jnp.int32, (rows, BLOCK), 0)
    low = low_ref[...]

    def tile(source, _):
        for step in range(2):
            for half in range(2):
                at = (step * 2 + half) * rows
                value = q_ref[source, step, :, half * HD : (half + 1) * HD].astype(jnp.float32)
                rotated[at : at + rows, :] = turn(value, cosine, sine).astype(jnp.bfloat16)
        maxima[...] = jnp.full(maxima.shape, NEG, jnp.float32)

        def score(block, _):
            start = pl.multiple_of(block * BLOCK, BLOCK)
            found = lax.dot_general(
                rotated[...],
                keys[pl.ds(start, BLOCK), :],
                (((1,), (1,)), ((), ())),
                preferred_element_type=jnp.float32,
            )
            whole = (start >= low_last) & (start + BLOCK - 1 <= first)

            @pl.when(whole)
            def _():
                scores[block] = found
                best = maxima[...]
                for part in range(BLOCK // HD):
                    best = jnp.maximum(best, found[:, part * HD : (part + 1) * HD])
                maxima[...] = best

            @pl.when(jnp.logical_not(whole))
            def _():
                key = start + lax.broadcasted_iota(jnp.int32, (rows, BLOCK), 1)
                allowed = (key <= token) & (key >= low)
                for index in range(4):
                    at = slice(index * rows, (index + 1) * rows)
                    masked = jnp.where(allowed, found[at, :], NEG)
                    scores[block, at, :] = masked
                    best = maxima[at, :]
                    for part in range(BLOCK // HD):
                        best = jnp.maximum(best, masked[:, part * HD : (part + 1) * HD])
                    maxima[at, :] = best

            return 0

        lax.fori_loop(begin, end, score, 0)
        best = jnp.max(maxima[...], axis=1, keepdims=True)
        k1 = k1_ref[...].astype(jnp.float32)
        diagonal = jnp.sum(
            rotated[2 * rows :, :].astype(jnp.float32).reshape(2, rows, HD) * k1[None], axis=-1, keepdims=True
        ).reshape(2 * rows, 1)
        best = jnp.concatenate([best[: 2 * rows], jnp.maximum(best[2 * rows :], diagonal)], axis=0)
        shifted = best * to_two

        def weigh(block, total):
            start = pl.multiple_of(block * BLOCK, BLOCK)
            weights = jnp.exp2(scores[block] * to_two - shifted).astype(jnp.bfloat16)
            return total + jnp.dot(weights, values[pl.ds(start, BLOCK), :], preferred_element_type=jnp.float32)

        total = lax.fori_loop(begin, end, weigh, jnp.zeros((4 * rows, 2 * HD), jnp.float32))
        accum, count = total[:, :HD], total[:, HD:]
        own = jnp.exp2(diagonal * to_two - shifted[2 * rows :])
        v1 = v1_ref[...].astype(jnp.float32)
        own_round = own.astype(jnp.bfloat16).astype(jnp.float32)
        extra = (own_round.reshape(2, rows, 1) * v1[None]).reshape(2 * rows, HD)
        for step in range(2):
            for half in range(2):
                index = step * 2 + half
                at = slice(index * rows, (index + 1) * rows)
                top, below = accum[at], count[at]
                if step == 1:
                    here = slice(half * rows, (half + 1) * rows)
                    top, below = top + extra[here], below + own[here]
                column = pl.multiple_of(source * 2 * HD, 2 * HD) + half * HD
                out_ref[step, :, pl.ds(column, HD)] = (top / below).astype(jnp.bfloat16)
        return 0

    lax.fori_loop(0, 4, tile, 0)


def attend(info, queries, cosine, sine, low, kv1, blocks):
    rows = low.shape[0]
    whole = lambda h: (0, 0)
    key_col = lambda h: (0, h)
    value_col = lambda h: (0, KVH + h)
    length = 256 * len(blocks)
    return pl.pallas_call(
        attend_body,
        out_shape=jax.ShapeDtypeStruct((2, rows, QH * HD), jnp.bfloat16),
        grid=(KVH,),
        in_specs=[
            pl.BlockSpec(memory_space=pltpu.SMEM),
            pl.BlockSpec((4, 2, rows, 2 * HD), lambda h: (h, 0, 0, 0)),
            pl.BlockSpec((rows, HD), whole),
            pl.BlockSpec((rows, HD), whole),
            pl.BlockSpec((rows, 1), whole),
            pl.BlockSpec((rows, HD), key_col),
            pl.BlockSpec((rows, HD), value_col),
        ]
        + [pl.BlockSpec((256, HD), key_col)] * 8
        + [pl.BlockSpec((256, HD), value_col)] * 8,
        out_specs=pl.BlockSpec((2, rows, 8 * HD), lambda h: (0, 0, h)),
        scratch_shapes=[
            pltpu.VMEM((length, HD), jnp.bfloat16),
            pltpu.VMEM((length, 2 * HD), jnp.bfloat16),
            pltpu.VMEM((length // BLOCK, 4 * rows, BLOCK), jnp.float32),
            pltpu.VMEM((4 * rows, HD), jnp.float32),
            pltpu.VMEM((4 * rows, HD), jnp.bfloat16),
        ],
        compiler_params=pltpu.CompilerParams(vmem_limit_bytes=VMEM),
        name="attend",
    )(info, queries, cosine, sine, low, kv1, kv1, *blocks, *blocks)


def on_device(hidden, norm_gain, kv_weight, queries, positions):
    steps, rows, width = hidden.shape
    grp, tp = lax.axis_index("grp"), lax.axis_index("tp")
    x, y, z, core = coords(grp, tp)
    where = jnp.stack([x, y, z, core]).astype(jnp.int32)

    sent = queries.reshape(steps, 16, rows, 2 * HD).transpose(1, 0, 2, 3)
    local_queries = lax.all_to_all(sent, "tp", split_axis=0, concat_axis=0, tiled=True)

    along = jnp.stack(ring8(kv_weight))
    first_a = ring4(along[:, :, :COLS_A], "dy")
    first_b = ring4(along[:, :, COLS_A:], "dx")

    def joined(found):
        return jnp.stack([found[0], found[1], found[2], jnp.concatenate([found[3], found[4]])])

    pieces_a = ring4(joined(first_a), "dx")
    pieces_b = ring4(joined(first_b), "dy")

    mine, other = norm(hidden.reshape(steps * rows, width), norm_gain[None, :], where[3:])
    other = shift(other, swap=True)

    freqs = rope_base ** (-jnp.arange(HD // 2, dtype=jnp.float32) * 2.0 / HD)
    angles = positions.astype(jnp.float32)[:, None] * freqs[None, :]
    cosine, sine = jnp.cos(angles), jnp.sin(angles)
    cosine = jnp.concatenate([cosine, cosine], axis=-1)
    sine = jnp.concatenate([-sine, sine], axis=-1)

    projected = project(where[:3], mine, other, pieces_a, pieces_b)
    got = shift(projected[steps * rows :], swap=True)
    kv0, kv1 = keys_values(projected[: steps * rows], got, cosine, sine)

    partner = shift(kv0, dy=2)
    pair = jnp.where(tp % 2 == 0, jnp.concatenate([kv0, partner]), jnp.concatenate([partner, kv0]))
    blocks = ring8(pair)

    first = (tp * rows).astype(jnp.int32)
    low = first + jnp.arange(rows, dtype=jnp.int32) - positions
    info = jnp.stack([z.astype(jnp.int32), first, low[0], low[rows - 1]])
    return attend(info, local_queries, cosine, sine, low[:, None], kv1, blocks)


def solution(mesh):
    placed = (
        P(None, ("grp", "tp"), None),
        P(),
        P(("grp", "tp"), None),
        P(None, "grp", "tp"),
        P(("grp", "tp")),
    )
    return jax.shard_map(
        on_device,
        mesh=mesh,
        in_specs=placed,
        out_specs=P(None, ("grp", "tp"), None),
        check_vma=False,
    )
```

```python
import functools
import math

import jax
import jax.numpy as jnp
from jax import lax
from jax.experimental import pallas as pl
from jax.experimental.pallas import tpu as pltpu
from jax.sharding import PartitionSpec as P

HD = 128
QH = 32
KVH = 4
BOTH = ("grp", "tp")
COLS_A = 512
COLS_B = 512
N_A, N_B = COLS_A // 128 * 8, COLS_B // 128 * 8
H_A, H_B = N_A // 2, N_B // 2
PAIR = 256
TILE = 256
VMEM = 40 * 1024 * 1024
VMEM_ATTEND = 16 * 1024 * 1024
NEG = -1e30
rope_base = 500000.0


def coords(grp, tp):
    return grp // 4, (tp % 2) * 2 + (grp // 2) % 2, tp // 2, grp % 2


def place(x, y, z, core):
    return ((x * 2 + y % 2) * 2 + core) * 16 + z * 2 + y // 2


def shift(value, dx=0, dy=0, dz=0, swap=False):
    pairs = []
    for device in range(256):
        x, y, z, core = coords(device // 16, device % 16)
        target = place((x + dx) % 4, (y + dy) % 4, (z + dz) % 8, 1 - core if swap else core)
        pairs.append((device, target))
    return lax.ppermute(value, BOTH, pairs)


def params(flops=0, moved=0, exps=0, vmem=VMEM):
    return dict(
        compiler_params=pltpu.CompilerParams(vmem_limit_bytes=vmem),
        cost_estimate=pl.CostEstimate(flops=flops, bytes_accessed=moved, transcendentals=exps),
    )


def ring8(block):
    up, down = shift(block, dz=1), shift(block, dz=-1)
    found = [(0, block), (-1, up), (1, down)]
    for step in (2, 3):
        up, down = shift(up, dz=1), shift(down, dz=-1)
        found += [(-step, up), (step, down)]
    return found, up, down


def arrange_body(where_ref, *refs):
    a_ref, b_ref = refs[8:]
    z0 = where_ref[2]
    for off, ref in zip((0, -1, 1, -2, 2, -3, 3, -4), refs[:8]):
        z = (z0 + off + 8) % 8
        for part in range(8):
            block = ref[:, part * 128 : (part + 1) * 128]
            if part * 128 < COLS_A:
                a_ref[part * 8 + z] = block
            else:
                b_ref[part * 8 - N_A + z] = block


def blocks_of(count):
    return jax.ShapeDtypeStruct((count, 32, 128), jnp.bfloat16)


def arrange(where, pieces):
    vmem = pl.BlockSpec(memory_space=pltpu.VMEM)
    return pl.pallas_call(
        arrange_body,
        out_shape=(blocks_of(N_A), blocks_of(N_B)),
        in_specs=[pl.BlockSpec(memory_space=pltpu.SMEM)] + [vmem] * 8,
        out_specs=(vmem, vmem),
        name="arrange",
        **params(moved=1 << 20),
    )(where, *pieces)


def pack(name, arrays, *plans):
    vmem = pl.BlockSpec(memory_space=pltpu.VMEM)

    def body(*refs):
        for plan, out_ref in zip(plans, refs[len(arrays) :]):
            at = 0
            for number, begin, end in plan:
                out_ref[at : at + end - begin] = refs[number][begin:end]
                at += end - begin

    return pl.pallas_call(
        body,
        out_shape=tuple(blocks_of(sum(end - begin for _, begin, end in plan)) for plan in plans),
        in_specs=[vmem] * len(arrays),
        out_specs=(vmem,) * len(plans),
        name=name,
        **params(moved=4 << 20),
    )(*arrays)


def both_ways(up, down, axis):
    return shift(up, **{axis: 1}), shift(down, **{axis: -1})


def norm_body(core_ref, hidden_ref, gain_ref, mine_ref, other_ref):
    core = core_ref[0]
    wide = hidden_ref[...].astype(jnp.float32)
    scale = lax.rsqrt(jnp.mean(wide * wide, axis=-1, keepdims=True) + 1e-05)
    for group in range(8):
        for out_ref, which in ((mine_ref, core), (other_ref, 1 - core)):
            start = pl.multiple_of((2 * group + which) * 512, 512)
            part = hidden_ref[:, pl.ds(start, 512)].astype(jnp.float32)
            gain = gain_ref[:, pl.ds(start, 512)]
            out_ref[:, group * 512 : (group + 1) * 512] = (part * scale * gain).astype(jnp.bfloat16)


def norm(hidden, gain, core):
    rows, width = hidden.shape
    out = jax.ShapeDtypeStruct((rows, width // 2), jnp.bfloat16)
    return pl.pallas_call(
        norm_body,
        out_shape=(out, out),
        grid=(rows // 64,),
        in_specs=[
            pl.BlockSpec(memory_space=pltpu.SMEM),
            pl.BlockSpec((64, width), lambda i: (i, 0)),
            pl.BlockSpec((1, width), lambda i: (0, 0)),
        ],
        out_specs=(
            pl.BlockSpec((64, width // 2), lambda i: (i, 0)),
            pl.BlockSpec((64, width // 2), lambda i: (i, 0)),
        ),
        compiler_params=pltpu.CompilerParams(vmem_limit_bytes=VMEM),
        name="norm",
    )(core, hidden, gain)


def segments(count, pieces):
    at = 0
    for ref, begin, blocks in pieces:
        while blocks:
            run = min(blocks, 8 - at % 8)
            yield ref, begin, at // 8 * 128, at % 8, run
            at, begin, blocks = at + run, begin + run, blocks - run
    assert at == count


class Puts:
    def __init__(self, where_ref, sems, weight_a, weight_b):
        self.x, self.y, self.sems, self.weight_a, self.weight_b = where_ref[0], where_ref[1], sems, weight_a, weight_b
        self.copies = []

    def start(self, source, target):
        copy = pltpu.make_async_copy(source, target, self.sems.at[len(self.copies)])
        copy.start()
        self.copies.append(copy)

    def wait(self, begin, end):
        for copy in self.copies[begin:end]:
            copy.wait()

    def a(self, slot, off_y, *pieces):
        y = (self.y + off_y + 4) % 4
        for ref, begin, col, z, run in segments(N_A, pieces):
            target = self.weight_a.at[slot, y % 2, pl.ds(z, run), y // 2, :, pl.ds(col, 128)]
            self.start(ref.at[pl.ds(begin, run)], target)

    def b(self, off_x, off_y, *pieces):
        x, y = (self.x + off_x + 4) % 4, (self.y + off_y + 4) % 4
        for ref, begin, col, z, run in segments(N_B, pieces):
            target = self.weight_b.at[x, pl.ds(z, run), y // 2, :, pl.ds(col, 128)]
            self.start(ref.at[pl.ds(begin, run)], target)


def times_a(where_ref, rows_ref, weight, offsets):
    total = None
    for slot, off in enumerate(offsets):
        x = (where_ref[0] + off + 4) % 4
        lhs = rows_ref[:, pl.ds(pl.multiple_of(x * 1024, 1024), 1024)]
        part = jnp.dot(lhs, weight[slot].reshape(1024, COLS_A), preferred_element_type=jnp.float32)
        total = part if total is None else total + part
    return total


def times_b(where_ref, rows_ref, weight, low):
    total = None
    for x in range(4):
        lhs = rows_ref[:, pl.ds(pl.multiple_of((x * 2 + low) * 512, 512), 512)]
        part = jnp.dot(lhs, weight[x].reshape(512, weight.shape[-1]), preferred_element_type=jnp.float32)
        total = part if total is None else total + part
    return total


def project_near_body(where_ref, mine_ref, other_ref, *refs):
    own_a, up_a, down_a, up2_x, down2_x, up3_x, down3_x, up2_y, down2_y, up3_y, down3_y = refs[:11]
    mine_out, other_out, weight_a, weight_b, sems = refs[11:]
    puts = Puts(where_ref, sems, weight_a, weight_b)
    puts.a(0, 0, (own_a, 0, N_A))
    puts.a(0, -1, (up_a, 0, N_A))
    puts.a(0, 1, (down_a, 0, N_A))
    puts.a(0, -2, (up2_y, 0, H_A), (down2_y, 0, H_A))
    for slot, second, third in ((1, up2_x, up3_x), (2, down2_x, down3_x)):
        puts.a(slot, 0, (second, H_B, N_A))
        puts.a(slot, -1, (second, H_B + N_A, N_A))
        puts.a(slot, 1, (third, 0, N_A))
        puts.a(slot, -2, (third, N_A, N_A))
    half = len(puts.copies)
    for off, second, third in ((-1, up2_y, up3_y), (1, down2_y, down3_y)):
        puts.b(0, off, (second, H_A, N_B))
        puts.b(-1, off, (second, H_A + N_B, N_B))
        puts.b(1, off, (third, 0, N_B))
        puts.b(-2, off, (third, N_B, N_B))
    low = 1 - where_ref[1] % 2
    puts.wait(0, half)
    for rows_ref, out_ref in ((mine_ref, mine_out), (other_ref, other_out)):
        out_ref[:, :COLS_A] = times_a(where_ref, rows_ref, weight_a, (0, -1, 1))
    puts.wait(half, None)
    for rows_ref, out_ref in ((mine_ref, mine_out), (other_ref, other_out)):
        out_ref[:, COLS_A:] = times_b(where_ref, rows_ref, weight_b, low)


def project_far_body(where_ref, mine_ref, other_ref, *refs):
    own_b, up_b, down_b, up2_x, down2_x, up3_x, down3_x, up4_x, down4_x, up3_y, down3_y, up4_y, down4_y = refs[:13]
    mine_part, other_part, mine_out, other_out, weight_a, weight_b, sems = refs[13:]
    puts = Puts(where_ref, sems, weight_a, weight_b)
    puts.a(0, 0, (up3_x, 2 * N_A, N_A))
    puts.a(0, -1, (down3_x, 2 * N_A, N_A))
    puts.a(0, 1, (up4_x, 0, N_A))
    puts.a(0, -2, (down4_x, 0, N_A))
    half = len(puts.copies)
    puts.b(0, 0, (own_b, 0, N_B))
    puts.b(-1, 0, (up_b, 0, N_B))
    puts.b(1, 0, (down_b, 0, N_B))
    puts.b(-2, 0, (up2_x, 0, H_B), (down2_x, 0, H_B))
    puts.b(0, -2, (up3_y, 2 * N_B, N_B))
    puts.b(-1, -2, (down3_y, 2 * N_B, N_B))
    puts.b(1, -2, (up4_y, 0, N_B))
    puts.b(-2, -2, (down4_y, 0, N_B))
    low = where_ref[1] % 2
    both = ((other_ref, other_part, other_out), (mine_ref, mine_part, mine_out))
    puts.wait(0, half)
    for rows_ref, part_ref, out_ref in both:
        out_ref[:, :COLS_A] = part_ref[:, :COLS_A] + times_a(where_ref, rows_ref, weight_a, (-2,))
    puts.wait(half, None)
    for rows_ref, part_ref, out_ref in both:
        out_ref[:, COLS_A:] = part_ref[:, COLS_A:] + times_b(where_ref, rows_ref, weight_b, low)


def project(body, name, slots, where, mine, other, pieces, parts=()):
    rows = mine.shape[0]
    out = pltpu.VMEM((rows, COLS_A + COLS_B), jnp.float32)
    vmem = pl.BlockSpec(memory_space=pltpu.VMEM)
    hbm = pl.BlockSpec(memory_space=pl.ANY)
    return pl.pallas_call(
        body,
        out_shape=(out, out if not parts else jax.ShapeDtypeStruct(out.shape, out.dtype)),
        in_specs=[pl.BlockSpec(memory_space=pltpu.SMEM)] + [vmem] * 2 + [hbm] * len(pieces) + [vmem] * len(parts),
        out_specs=(vmem, vmem),
        scratch_shapes=[
            pltpu.VMEM((slots, 2, 8, 2, 32, COLS_A), jnp.bfloat16),
            pltpu.VMEM((4, 8, 2, 32, COLS_B), jnp.bfloat16),
            pltpu.SemaphoreType.DMA((128,)),
        ],
        name=name,
        **params(flops=1 << 31, moved=12 << 20),
    )(where, mine, other, *pieces, *parts)


def turn(values, cosine, sine):
    return values * cosine + pltpu.roll(values, 64, 1) * sine


def split_body(where_ref, q_ref, keep_ref, low_ref, high_ref):
    y_hi, z = where_ref[1] // 2, pl.program_id(0)
    keep_ref[0] = q_ref[:, 0, y_hi]

    @pl.when(z < 4)
    def _():
        low_ref[0] = q_ref[:, 0, 1 - y_hi]

    @pl.when(z >= 4)
    def _():
        high_ref[0] = q_ref[:, 0, 1 - y_hi]


def split(where, queries, rows):
    steps = queries.shape[0]
    shape = (steps, rows, 2 * HD)
    block = (1, *shape)
    return pl.pallas_call(
        split_body,
        out_shape=tuple(jax.ShapeDtypeStruct((count, *shape), jnp.bfloat16) for count in (8, 4, 4)),
        grid=(8,),
        in_specs=[
            pl.BlockSpec(memory_space=pltpu.SMEM),
            pl.BlockSpec((steps, 1, 2, rows, 2 * HD), lambda z: (0, z, 0, 0, 0)),
        ],
        out_specs=(
            pl.BlockSpec(block, lambda z: (z, 0, 0, 0)),
            pl.BlockSpec(block, lambda z: (jnp.minimum(z, 3), 0, 0, 0)),
            pl.BlockSpec(block, lambda z: (jnp.maximum(z, 4) - 4, 0, 0, 0)),
        ),
        name="split",
        **params(moved=4 << 20),
    )(where, queries.reshape(steps, 8, 2, rows, 2 * HD))


def rotate_body(where_ref, q_ref, cos_ref, sin_ref, out_ref):
    rows = cos_ref.shape[0]
    cosine, sine = cos_ref[...], sin_ref[...]
    y_hi, head = where_ref[1] // 2, pl.program_id(0)
    for low_z in range(2):
        for other in range(2):
            source = 2 * low_z + (y_hi if other == 0 else 1 - y_hi)
            for step in range(2):
                for half in range(2):
                    at = pl.multiple_of((source * 4 + step * 2 + half) * rows, rows)
                    value = q_ref[low_z, other, step, :, half * HD : (half + 1) * HD].astype(jnp.float32)
                    out_ref[head, pl.ds(at, rows), :] = turn(value, cosine, sine).astype(jnp.bfloat16)


def rotate(where, queries, cosine, sine):
    rows = cosine.shape[0]
    whole = lambda h: (0, 0)
    return pl.pallas_call(
        rotate_body,
        out_shape=pltpu.VMEM((KVH, 16 * rows, HD), jnp.bfloat16),
        grid=(KVH,),
        in_specs=[
            pl.BlockSpec(memory_space=pltpu.SMEM),
            pl.BlockSpec((2, 2, 2, rows, 2 * HD), lambda h: (h, 0, 0, 0, 0)),
            pl.BlockSpec((rows, HD), whole),
            pl.BlockSpec((rows, HD), whole),
        ],
        out_specs=pl.BlockSpec(memory_space=pltpu.VMEM),
        name="rotate",
        **params(flops=1 << 23, moved=4 << 20),
    )(where, queries, cosine, sine)


def keys_values_body(own_ref, got_ref, cos_ref, sin_ref, low_ref, high_ref, second_ref):
    rows = second_ref.shape[0]
    cosine, sine = cos_ref[...], sin_ref[...]
    for step in range(2):
        for head in range(2 * KVH):
            cols = slice(head * HD, (head + 1) * HD)
            part = own_ref[step * rows : (step + 1) * rows, cols]
            part = part + got_ref[step * rows : (step + 1) * rows, cols]
            if head < KVH:
                part = turn(part, cosine, sine)
            part = part.astype(jnp.bfloat16)
            if step == 0:
                low_ref[:, cols] = part[: rows // 2]
                high_ref[:, cols] = part[rows // 2 :]
            else:
                second_ref[:, cols] = part


def keys_values(own, got, cosine, sine):
    rows, cols = own.shape
    half = jax.ShapeDtypeStruct((rows // 4, cols), jnp.bfloat16)
    vmem = pl.BlockSpec(memory_space=pltpu.VMEM)
    return pl.pallas_call(
        keys_values_body,
        out_shape=(half, half, jax.ShapeDtypeStruct((rows // 2, cols), jnp.bfloat16)),
        in_specs=[vmem] * 4,
        out_specs=(vmem, vmem, vmem),
        name="keys_values",
        **params(flops=1 << 20, moved=4 << 20),
    )(own, got, cosine, sine)


def join(*parts):
    rows, cols = parts[0].shape
    vmem = pl.BlockSpec(memory_space=pltpu.VMEM)

    def body(*refs):
        for index, ref in enumerate(refs[:-1]):
            refs[-1][index * rows : (index + 1) * rows, :] = ref[...]

    return pl.pallas_call(
        body,
        out_shape=jax.ShapeDtypeStruct((rows * len(parts), cols), parts[0].dtype),
        in_specs=[vmem] * len(parts),
        out_specs=vmem,
        name="join",
        **params(moved=1 << 20),
    )(*parts)


def attend_body(offsets, is_first, is_last, info_ref, low_ref, q_ref, *refs):
    count = len(offsets)
    k_refs, v_refs, refs = refs[:count], refs[count : 2 * count], refs[2 * count :]
    if is_first:
        (k1_ref, v1_ref), refs = refs[:2], refs[2:]
    else:
        (sum_in, max_in), refs = refs[:2], refs[2:]
    if is_last:
        (out_ref, sum_out, max_out), refs = (refs[0], sum_in, max_in), refs[1:]
    else:
        (sum_out, max_out), refs = refs[:2], refs[2:]
    keys, values, bias = refs
    z0, y_hi, first = info_ref[0], info_ref[1], info_ref[2]
    low_first, low_last = info_ref[3], info_ref[4]
    rows = low_ref.shape[0]
    head = pl.program_id(0)
    total_rows = q_ref.shape[1]
    width = count * PAIR
    to_two = math.log2(math.e) / math.sqrt(HD)

    needed, whole, starts = False, True, []
    for off in offsets:
        z = (z0 + off + 8) % 8
        start = z * PAIR
        starts.append(start)
        needed = needed | ((z <= z0) & (start + PAIR - 1 >= low_first))
        whole = whole & (z < z0) & (start >= low_last)

    for index in range(count):
        at = slice(index * PAIR, (index + 1) * PAIR)
        keys[at, :] = k_refs[index][...]
        values[at, :HD] = v_refs[index][...]
    values[:, HD:] = jnp.ones((width, HD), jnp.bfloat16)

    def tile(at, biased):
        scores = lax.dot_general(
            q_ref[head, at, :], keys[...], (((1,), (1,)), ((), ())), preferred_element_type=jnp.float32
        )
        if biased:
            scores = (scores.reshape(TILE // rows, rows, width) + bias[...][None]).reshape(TILE, width)
        best = scores[:, :HD]
        for part in range(1, width // HD):
            best = jnp.maximum(best, scores[:, part * HD : (part + 1) * HD])
        best = jnp.broadcast_to(jnp.max(best, axis=1, keepdims=True), (TILE, HD))
        if is_first:
            index = at.start // rows
            if (index // 2) % 2 == 1:
                q = q_ref[head, at, :].astype(jnp.float32).reshape(TILE // rows, rows, HD)
                diagonal = jnp.sum(q * k1_ref[...].astype(jnp.float32)[None], axis=-1, keepdims=True)
                old = jnp.broadcast_to(diagonal, (TILE // rows, rows, HD)).reshape(TILE, HD)
                value = v1_ref[...].astype(jnp.float32)
                begin = jnp.concatenate([value] * (TILE // rows), axis=0), jnp.ones((TILE, HD), jnp.float32)
            else:
                old, begin = None, None
        else:
            old = max_in[head, at, :]
            begin = sum_in[head, at, :HD], sum_in[head, at, HD:]
        new = best if old is None else jnp.maximum(old, best)
        shifted = new * to_two
        weights = jnp.concatenate(
            [
                jnp.exp2(scores[:, part * HD : (part + 1) * HD] * to_two - shifted).astype(jnp.bfloat16)
                for part in range(width // HD)
            ],
            axis=1,
        )
        found = jnp.dot(weights, values[...], preferred_element_type=jnp.float32)
        if old is None:
            sum_out[head, at, :] = found
        else:
            factor = jnp.exp2(old * to_two - shifted)
            sum_out[head, at, :HD] = begin[0] * factor + found[:, :HD]
            sum_out[head, at, HD:] = begin[1] * factor + found[:, HD:]
        max_out[head, at, :] = new

    def run(biased):
        for start in range(0, total_rows, TILE):
            tile(slice(start, start + TILE), biased)

    def set_bias():
        token = first + lax.broadcasted_iota(jnp.int32, (rows, PAIR), 0)
        lane = lax.broadcasted_iota(jnp.int32, (rows, PAIR), 1)
        inside = (lane + y_hi * (PAIR // 2)) & (PAIR - 1)
        for index, start in enumerate(starts):
            key = start + inside
            allowed = (key <= token) & (key >= low_ref[...])
            bias[:, index * PAIR : (index + 1) * PAIR] = jnp.where(allowed, 0.0, NEG)

    if is_first:
        set_bias()
        run(True)
    else:

        @pl.when(whole)
        def _():
            run(False)

        @pl.when(needed & jnp.logical_not(whole))
        def _():
            set_bias()
            run(True)

    if is_last:
        for index in range(total_rows // rows):
            source, step, half = index // 4, (index // 2) % 2, index % 2
            at = slice(index * rows, (index + 1) * rows)
            column = (source * 2 + half) * HD
            result = sum_out[head, at, :HD] / sum_out[head, at, HD:]
            out_ref[step, :, column : column + HD] = result.astype(jnp.bfloat16)


def attend(info, low, rotated, pieces, kv1=None, state=None, is_last=False):
    is_first = state is None
    offsets = tuple(off for off, _ in pieces)
    blocks = [block for _, block in pieces]
    count = len(blocks)
    total_rows = rotated.shape[1]
    rows = low.shape[0]
    whole = lambda h: (0, 0)
    key_col = lambda h: (0, h)
    value_col = lambda h: (0, KVH + h)
    sums = pltpu.VMEM((KVH, total_rows, 2 * HD), jnp.float32)
    maxima = pltpu.VMEM((KVH, total_rows, HD), jnp.float32)
    state_specs = [pl.BlockSpec(memory_space=pltpu.VMEM)] * 2
    in_specs = [
        pl.BlockSpec(memory_space=pltpu.SMEM),
        pl.BlockSpec((rows, 1), whole),
        pl.BlockSpec(memory_space=pltpu.VMEM),
    ]
    in_specs += [pl.BlockSpec((PAIR, HD), key_col)] * count + [pl.BlockSpec((PAIR, HD), value_col)] * count
    scratch = [
        pltpu.VMEM((count * PAIR, HD), jnp.bfloat16),
        pltpu.VMEM((count * PAIR, 2 * HD), jnp.bfloat16),
        pltpu.VMEM((rows, count * PAIR), jnp.float32),
    ]
    operands = [info, low, rotated, *blocks, *blocks]
    if is_first:
        in_specs += [pl.BlockSpec((rows, HD), key_col), pl.BlockSpec((rows, HD), value_col)]
        operands += [kv1, kv1]
    else:
        in_specs += state_specs
        operands += list(state)
    if is_last:
        out_shape = jax.ShapeDtypeStruct((2, rows, QH * HD), jnp.bfloat16)
        out_specs = pl.BlockSpec((2, rows, 8 * HD), lambda h: (0, 0, h))
        aliases = {}
    else:
        out_shape, out_specs = (sums, maxima), tuple(state_specs)
        aliases = {} if is_first else {len(operands) - 2: 0, len(operands) - 1: 1}
    return pl.pallas_call(
        functools.partial(attend_body, offsets, is_first, is_last),
        out_shape=out_shape,
        grid=(KVH,),
        in_specs=in_specs,
        out_specs=out_specs,
        scratch_shapes=scratch,
        input_output_aliases=aliases,
        name="attend_first" if is_first else "attend_last" if is_last else "attend_next",
        **params(
            flops=4 * KVH * total_rows * count * PAIR * 2 * HD,
            moved=24 << 20,
            exps=KVH * total_rows * count * PAIR,
            vmem=VMEM_ATTEND,
        ),
    )(*operands)


def on_device(hidden, norm_gain, kv_weight, queries, positions):
    steps, rows, width = hidden.shape
    grp, tp = lax.axis_index("grp"), lax.axis_index("tp")
    x, y, z, core = coords(grp, tp)
    where = jnp.stack([x, y, z, core]).astype(jnp.int32)

    found, up, _ = ring8(kv_weight)
    found = [block for _, block in found] + [shift(up, dz=1)]
    along_a, along_b = arrange(where, found)
    up_a, down_a = both_ways(along_a, along_a, "dy")
    up_b, down_b = both_ways(along_b, along_b, "dx")

    x_up, x_down, y_up, y_down = pack(
        "pack_low",
        (along_a, up_a, down_a, along_b, up_b, down_b),
        ((4, 0, H_B), (0, 0, N_A), (1, 0, N_A)),
        ((5, H_B, N_B), (0, 0, N_A), (1, 0, N_A)),
        ((1, 0, H_A), (3, 0, N_B), (4, 0, N_B)),
        ((2, H_A, N_A), (3, 0, N_B), (4, 0, N_B)),
    )
    low_x = x_up
    up2_x, down2_x = both_ways(x_up, x_down, "dx")
    up2_y, down2_y = both_ways(y_up, y_down, "dy")

    x_up, x_down, y_up, y_down = pack(
        "pack_high",
        (down_a, down_b, up2_x, down2_x, up2_y, down2_y),
        ((0, 0, N_A), (4, 0, H_A), (5, 0, H_A), (2, H_B, H_B + N_A)),
        ((0, 0, N_A), (4, 0, H_A), (5, 0, H_A), (3, H_B + N_A, H_B + 2 * N_A)),
        ((1, 0, N_B), (2, 0, H_B), (3, 0, H_B), (4, H_A, H_A + N_B)),
        ((1, 0, N_B), (2, 0, H_B), (3, 0, H_B), (5, H_A + N_B, H_A + 2 * N_B)),
    )
    up3_x, down3_x = both_ways(x_up, x_down, "dx")
    up3_y, down3_y = both_ways(y_up, y_down, "dy")

    x_up, x_down, y_up, y_down = pack(
        "pack_far",
        (up3_x, down3_x, up3_y, down3_y),
        ((0, 0, N_A),),
        ((1, N_A, 2 * N_A),),
        ((2, 0, N_B),),
        ((3, N_B, 2 * N_B),),
    )
    up4_x, down4_x = both_ways(x_up, x_down, "dx")
    up4_y, down4_y = both_ways(y_up, y_down, "dy")

    keep, low, high = split(where, queries, rows)
    low, high = shift(low, dy=1), shift(high, dy=-1)
    got = jnp.concatenate([shift(low, dy=1), shift(high, dy=-1)])
    sent, _ = lax.optimization_barrier((jnp.stack([keep, got], axis=1), along_a))
    local_queries = lax.all_to_all(
        sent,
        "tp",
        split_axis=0,
        concat_axis=0,
        axis_index_groups=[list(range(0, 16, 2)), list(range(1, 16, 2))],
        tiled=True,
    )

    hidden, _ = lax.optimization_barrier((hidden, low_x))
    mine, other = norm(hidden.reshape(steps * rows, width), norm_gain[None, :], where[3:])
    other = shift(other, swap=True)

    freqs = rope_base ** (-jnp.arange(HD // 2, dtype=jnp.float32) * 2.0 / HD)
    angles = positions.astype(jnp.float32)[:, None] * freqs[None, :]
    cosine, sine = jnp.cos(angles), jnp.sin(angles)
    cosine = jnp.concatenate([cosine, cosine], axis=-1)
    sine = jnp.concatenate([-sine, sine], axis=-1)

    near = (along_a, up_a, down_a, up2_x, down2_x, up3_x, down3_x, up2_y, down2_y, up3_y, down3_y)
    parts = project(project_near_body, "project_near", 3, where, mine, other, near)
    far = (along_b, up_b, down_b, up2_x, down2_x, up3_x, down3_x, up4_x, down4_x, up3_y, down3_y, up4_y, down4_y)
    own, sent_part = project(project_far_body, "project_far", 1, where, mine, other, far, parts)
    got = shift(sent_part, swap=True)
    low_half, high_half, kv1 = keys_values(own, got, cosine, sine)

    first_up = shift(low_half, dy=1)
    first_down = shift(high_half, dy=-1)
    local_queries, _ = lax.optimization_barrier((local_queries, low_half))
    rotated = rotate(where, local_queries, cosine, sine)
    pair = join(low_half, high_half, shift(first_up, dy=1), shift(first_down, dy=-1))

    first = (tp * rows).astype(jnp.int32)
    low = first + jnp.arange(rows, dtype=jnp.int32) - positions
    info = jnp.stack([z.astype(jnp.int32), (tp % 2).astype(jnp.int32), first, low[0], low[rows - 1]])
    low = low[:, None]

    up, down = pair, pair
    state = attend(info, low, rotated, [(0, pair)], kv1=kv1)
    for step in (1, 2, 3):
        up, down = shift(up, dz=1), shift(down, dz=-1)
        up, down, *state = lax.optimization_barrier((up, down, *state))
        if step == 3:
            last = shift(up[: PAIR // 2], dz=1), shift(down[PAIR // 2 :], dz=-1)
        state = attend(info, low, rotated, [(-step, up), (step, down)], state=state)
    return attend(info, low, rotated, [(-4, jnp.concatenate(last))], state=state, is_last=True)


def solution(mesh):
    placed = (
        P(None, ("grp", "tp"), None),
        P(),
        P(("grp", "tp"), None),
        P(None, "grp", "tp"),
        P(("grp", "tp")),
    )
    return jax.shard_map(
        on_device,
        mesh=mesh,
        in_specs=placed,
        out_specs=P(None, ("grp", "tp"), None),
        check_vma=False,
    )
```

```python
import functools
import math

import jax
import jax.numpy as jnp
from jax import lax
from jax.experimental import pallas as pl
from jax.experimental.pallas import tpu as pltpu
from jax.sharding import PartitionSpec as P

HD = 128
QH = 32
KVH = 4
BOTH = ("grp", "tp")
COLS_A = 512
COLS_B = 512
N_A, N_B = COLS_A // 128 * 8, COLS_B // 128 * 8
H_A, H_B = N_A // 2, N_B // 2
PAIR = 256
TILE = 256
VMEM = 12 * 1024 * 1024
VMEM_PROJECT = 24 * 1024 * 1024
VMEM_ATTEND = 16 * 1024 * 1024
NEG = -1e30
rope_base = 500000.0


def coords(grp, tp):
    return grp // 4, (tp % 2) * 2 + (grp // 2) % 2, tp // 2, grp % 2


def place(x, y, z, core):
    return ((x * 2 + y % 2) * 2 + core) * 16 + z * 2 + y // 2


def shift(value, dx=0, dy=0, dz=0, swap=False):
    pairs = []
    for device in range(256):
        x, y, z, core = coords(device // 16, device % 16)
        target = place((x + dx) % 4, (y + dy) % 4, (z + dz) % 8, 1 - core if swap else core)
        pairs.append((device, target))
    return lax.ppermute(value, BOTH, pairs)


def params(flops=0, moved=0, exps=0, vmem=VMEM):
    return dict(
        compiler_params=pltpu.CompilerParams(vmem_limit_bytes=vmem),
        cost_estimate=pl.CostEstimate(flops=flops, bytes_accessed=moved, transcendentals=exps),
    )


def arrange_body(where_ref, *refs):
    a_ref, b_ref = refs[8:]
    z0 = where_ref[2]
    for off, ref in zip((0, -1, 1, -2, 2, -3, 3, -4), refs[:8]):
        z = (z0 + off + 8) % 8
        for part in range(8):
            block = ref[:, part * 128 : (part + 1) * 128]
            if part * 128 < COLS_A:
                a_ref[part * 8 + z] = block
            else:
                b_ref[part * 8 - N_A + z] = block


def blocks_of(count):
    return jax.ShapeDtypeStruct((count, 32, 128), jnp.bfloat16)


def arrange(where, pieces):
    vmem = pl.BlockSpec(memory_space=pltpu.VMEM)
    return pl.pallas_call(
        arrange_body,
        out_shape=(blocks_of(N_A), blocks_of(N_B)),
        in_specs=[pl.BlockSpec(memory_space=pltpu.SMEM)] + [vmem] * 8,
        out_specs=(vmem, vmem),
        name="arrange",
        **params(moved=1 << 20),
    )(where, *pieces)


def pack(name, arrays, *plans):
    vmem = pl.BlockSpec(memory_space=pltpu.VMEM)

    def body(*refs):
        for plan, out_ref in zip(plans, refs[len(arrays) :]):
            at = 0
            for number, begin, end in plan:
                out_ref[at : at + end - begin] = refs[number][begin:end]
                at += end - begin

    return pl.pallas_call(
        body,
        out_shape=tuple(blocks_of(sum(end - begin for _, begin, end in plan)) for plan in plans),
        in_specs=[vmem] * len(arrays),
        out_specs=(vmem,) * len(plans),
        name=name,
        **params(moved=4 << 20),
    )(*arrays)


def both_ways(up, down, axis):
    return shift(up, **{axis: 1}), shift(down, **{axis: -1})


def norm_body(core_ref, hidden_ref, gain_ref, mine_ref, other_ref):
    core = core_ref[0]
    wide = hidden_ref[...].astype(jnp.float32)
    scale = lax.rsqrt(jnp.mean(wide * wide, axis=-1, keepdims=True) + 1e-05)
    for group in range(8):
        for out_ref, which in ((mine_ref, core), (other_ref, 1 - core)):
            start = pl.multiple_of((2 * group + which) * 512, 512)
            part = hidden_ref[:, pl.ds(start, 512)].astype(jnp.float32)
            gain = gain_ref[:, pl.ds(start, 512)]
            out_ref[:, group * 512 : (group + 1) * 512] = (part * scale * gain).astype(jnp.bfloat16)


def norm(hidden, gain, core):
    rows, width = hidden.shape
    out = jax.ShapeDtypeStruct((rows, width // 2), jnp.bfloat16)
    return pl.pallas_call(
        norm_body,
        out_shape=(out, out),
        grid=(rows // 64,),
        in_specs=[
            pl.BlockSpec(memory_space=pltpu.SMEM),
            pl.BlockSpec((64, width), lambda i: (i, 0)),
            pl.BlockSpec((1, width), lambda i: (0, 0)),
        ],
        out_specs=(
            pl.BlockSpec((64, width // 2), lambda i: (i, 0)),
            pl.BlockSpec((64, width // 2), lambda i: (i, 0)),
        ),
        compiler_params=pltpu.CompilerParams(vmem_limit_bytes=VMEM),
        name="norm",
    )(core, hidden, gain)


def segments(count, pieces):
    at = 0
    for ref, begin, blocks in pieces:
        while blocks:
            run = min(blocks, 8 - at % 8)
            yield ref, begin, at // 8 * 128, at % 8, run
            at, begin, blocks = at + run, begin + run, blocks - run
    assert at == count


class Puts:
    def __init__(self, where_ref, sems, weight_a, weight_b):
        self.x, self.y, self.sems, self.weight_a, self.weight_b = where_ref[0], where_ref[1], sems, weight_a, weight_b
        self.copies = []

    def start(self, source, target):
        copy = pltpu.make_async_copy(source, target, self.sems.at[len(self.copies)])
        copy.start()
        self.copies.append(copy)

    def wait(self, begin, end):
        for copy in self.copies[begin:end]:
            copy.wait()

    def a(self, slot, off_y, *pieces):
        y = (self.y + off_y + 4) % 4
        for ref, begin, col, z, run in segments(N_A, pieces):
            target = self.weight_a.at[slot, y % 2, pl.ds(z, run), y // 2, :, pl.ds(col, 128)]
            self.start(ref.at[pl.ds(begin, run)], target)

    def b(self, off_x, off_y, *pieces):
        x, y = (self.x + off_x + 4) % 4, (self.y + off_y + 4) % 4
        for ref, begin, col, z, run in segments(N_B, pieces):
            target = self.weight_b.at[x, pl.ds(z, run), y // 2, :, pl.ds(col, 128)]
            self.start(ref.at[pl.ds(begin, run)], target)


def times_a(where_ref, rows_ref, weight, offsets):
    total = None
    for slot, off in enumerate(offsets):
        x = (where_ref[0] + off + 4) % 4
        lhs = rows_ref[:, pl.ds(pl.multiple_of(x * 1024, 1024), 1024)]
        part = jnp.dot(lhs, weight[slot].reshape(1024, COLS_A), preferred_element_type=jnp.float32)
        total = part if total is None else total + part
    return total


def times_b(where_ref, rows_ref, weight, low):
    total = None
    for x in range(4):
        lhs = rows_ref[:, pl.ds(pl.multiple_of((x * 2 + low) * 512, 512), 512)]
        part = jnp.dot(lhs, weight[x].reshape(512, weight.shape[-1]), preferred_element_type=jnp.float32)
        total = part if total is None else total + part
    return total


def project_near_body(where_ref, mine_ref, other_ref, *refs):
    own_a, up_a, down_a, up2_x, down2_x, up3_x, down3_x, up2_y, down2_y, up3_y, down3_y = refs[:11]
    mine_out, other_out, weight_a, weight_b, sems = refs[11:]
    puts = Puts(where_ref, sems, weight_a, weight_b)
    puts.a(0, 0, (own_a, 0, N_A))
    puts.a(0, -1, (up_a, 0, N_A))
    puts.a(0, 1, (down_a, 0, N_A))
    puts.a(0, -2, (up2_y, 0, H_A), (down2_y, 0, H_A))
    for slot, second, third in ((1, up2_x, up3_x), (2, down2_x, down3_x)):
        puts.a(slot, 0, (second, H_B, N_A))
        puts.a(slot, -1, (second, H_B + N_A, N_A))
        puts.a(slot, 1, (third, 0, N_A))
        puts.a(slot, -2, (third, N_A, N_A))
    half = len(puts.copies)
    for off, second, third in ((-1, up2_y, up3_y), (1, down2_y, down3_y)):
        puts.b(0, off, (second, H_A, N_B))
        puts.b(-1, off, (second, H_A + N_B, N_B))
        puts.b(1, off, (third, 0, N_B))
        puts.b(-2, off, (third, N_B, N_B))
    low = 1 - where_ref[1] % 2
    puts.wait(0, half)
    for rows_ref, out_ref in ((mine_ref, mine_out), (other_ref, other_out)):
        out_ref[:, :COLS_A] = times_a(where_ref, rows_ref, weight_a, (0, -1, 1))
    puts.wait(half, None)
    for rows_ref, out_ref in ((mine_ref, mine_out), (other_ref, other_out)):
        out_ref[:, COLS_A:] = times_b(where_ref, rows_ref, weight_b, low)


def project_far_body(where_ref, mine_ref, other_ref, *refs):
    own_b, up_b, down_b, up2_x, down2_x, up3_x, down3_x, up4_x, down4_x, up3_y, down3_y, up4_y, down4_y = refs[:13]
    mine_part, other_part, mine_out, other_out, weight_a, weight_b, sems = refs[13:]
    puts = Puts(where_ref, sems, weight_a, weight_b)
    puts.a(0, 0, (up3_x, 2 * N_A, N_A))
    puts.a(0, -1, (down3_x, 2 * N_A, N_A))
    puts.a(0, 1, (up4_x, 0, N_A))
    puts.a(0, -2, (down4_x, 0, N_A))
    half = len(puts.copies)
    puts.b(0, 0, (own_b, 0, N_B))
    puts.b(-1, 0, (up_b, 0, N_B))
    puts.b(1, 0, (down_b, 0, N_B))
    puts.b(-2, 0, (up2_x, 0, H_B), (down2_x, 0, H_B))
    puts.b(0, -2, (up3_y, 2 * N_B, N_B))
    puts.b(-1, -2, (down3_y, 2 * N_B, N_B))
    puts.b(1, -2, (up4_y, 0, N_B))
    puts.b(-2, -2, (down4_y, 0, N_B))
    low = where_ref[1] % 2
    both = ((other_ref, other_part, other_out), (mine_ref, mine_part, mine_out))
    puts.wait(0, half)
    for rows_ref, part_ref, out_ref in both:
        out_ref[:, :COLS_A] = part_ref[:, :COLS_A] + times_a(where_ref, rows_ref, weight_a, (-2,))
    puts.wait(half, None)
    for rows_ref, part_ref, out_ref in both:
        out_ref[:, COLS_A:] = part_ref[:, COLS_A:] + times_b(where_ref, rows_ref, weight_b, low)


def project(body, name, slots, where, mine, other, pieces, parts=()):
    rows = mine.shape[0]
    out = pltpu.VMEM((rows, COLS_A + COLS_B), jnp.float32)
    vmem = pl.BlockSpec(memory_space=pltpu.VMEM)
    hbm = pl.BlockSpec(memory_space=pl.ANY)
    return pl.pallas_call(
        body,
        out_shape=(out, out if not parts else jax.ShapeDtypeStruct(out.shape, out.dtype)),
        in_specs=[pl.BlockSpec(memory_space=pltpu.SMEM)] + [vmem] * 2 + [hbm] * len(pieces) + [vmem] * len(parts),
        out_specs=(vmem, vmem),
        scratch_shapes=[
            pltpu.VMEM((slots, 2, 8, 2, 32, COLS_A), jnp.bfloat16),
            pltpu.VMEM((4, 8, 2, 32, COLS_B), jnp.bfloat16),
            pltpu.SemaphoreType.DMA((128,)),
        ],
        name=name,
        **params(flops=1 << 31, moved=12 << 20, vmem=VMEM_PROJECT),
    )(where, mine, other, *pieces, *parts)


def turn(values, cosine, sine):
    return values * cosine + pltpu.roll(values, 64, 1) * sine


def split_body(where_ref, q_ref, keep_ref, low_ref, high_ref):
    y_hi, z = where_ref[1] // 2, pl.program_id(0)
    keep_ref[0] = q_ref[:, 0, y_hi]

    @pl.when(z < 4)
    def _():
        low_ref[0] = q_ref[:, 0, 1 - y_hi]

    @pl.when(z >= 4)
    def _():
        high_ref[0] = q_ref[:, 0, 1 - y_hi]


def split(where, queries, rows):
    steps = queries.shape[0]
    shape = (steps, rows, 2 * HD)
    block = (1, *shape)
    return pl.pallas_call(
        split_body,
        out_shape=tuple(jax.ShapeDtypeStruct((count, *shape), jnp.bfloat16) for count in (8, 4, 4)),
        grid=(8,),
        in_specs=[
            pl.BlockSpec(memory_space=pltpu.SMEM),
            pl.BlockSpec((steps, 1, 2, rows, 2 * HD), lambda z: (0, z, 0, 0, 0)),
        ],
        out_specs=(
            pl.BlockSpec(block, lambda z: (z, 0, 0, 0)),
            pl.BlockSpec(block, lambda z: (jnp.minimum(z, 3), 0, 0, 0)),
            pl.BlockSpec(block, lambda z: (jnp.maximum(z, 4) - 4, 0, 0, 0)),
        ),
        name="split",
        **params(moved=4 << 20),
    )(where, queries.reshape(steps, 8, 2, rows, 2 * HD))


def rotate_body(where_ref, q_ref, cos_ref, sin_ref, out_ref):
    rows = cos_ref.shape[0]
    cosine, sine = cos_ref[...], sin_ref[...]
    y_hi, head = where_ref[1] // 2, pl.program_id(0)
    for low_z in range(2):
        for other in range(2):
            source = 2 * low_z + (y_hi if other == 0 else 1 - y_hi)
            for step in range(2):
                for half in range(2):
                    at = pl.multiple_of((source * 4 + step * 2 + half) * rows, rows)
                    value = q_ref[low_z, other, step, :, half * HD : (half + 1) * HD].astype(jnp.float32)
                    out_ref[head, pl.ds(at, rows), :] = turn(value, cosine, sine).astype(jnp.bfloat16)


def rotate(where, queries, cosine, sine):
    rows = cosine.shape[0]
    whole = lambda h: (0, 0)
    return pl.pallas_call(
        rotate_body,
        out_shape=pltpu.VMEM((KVH, 16 * rows, HD), jnp.bfloat16),
        grid=(KVH,),
        in_specs=[
            pl.BlockSpec(memory_space=pltpu.SMEM),
            pl.BlockSpec((2, 2, 2, rows, 2 * HD), lambda h: (h, 0, 0, 0, 0)),
            pl.BlockSpec((rows, HD), whole),
            pl.BlockSpec((rows, HD), whole),
        ],
        out_specs=pl.BlockSpec(memory_space=pltpu.VMEM),
        name="rotate",
        **params(flops=1 << 23, moved=4 << 20),
    )(where, queries, cosine, sine)


def keys_values_body(own_ref, got_ref, cos_ref, sin_ref, low_ref, high_ref, second_ref):
    rows = second_ref.shape[0]
    cosine, sine = cos_ref[...], sin_ref[...]
    for step in range(2):
        for head in range(2 * KVH):
            cols = slice(head * HD, (head + 1) * HD)
            part = own_ref[step * rows : (step + 1) * rows, cols]
            part = part + got_ref[step * rows : (step + 1) * rows, cols]
            if head < KVH:
                part = turn(part, cosine, sine)
            part = part.astype(jnp.bfloat16)
            if step == 0:
                low_ref[:, cols] = part[: rows // 2]
                high_ref[:, cols] = part[rows // 2 :]
            else:
                second_ref[:, cols] = part


def keys_values(own, got, cosine, sine):
    rows, cols = own.shape
    half = jax.ShapeDtypeStruct((rows // 4, cols), jnp.bfloat16)
    vmem = pl.BlockSpec(memory_space=pltpu.VMEM)
    return pl.pallas_call(
        keys_values_body,
        out_shape=(half, half, jax.ShapeDtypeStruct((rows // 2, cols), jnp.bfloat16)),
        in_specs=[vmem] * 4,
        out_specs=(vmem, vmem, vmem),
        name="keys_values",
        **params(flops=1 << 20, moved=4 << 20),
    )(own, got, cosine, sine)


def join(*parts):
    rows, cols = parts[0].shape
    vmem = pl.BlockSpec(memory_space=pltpu.VMEM)

    def body(*refs):
        for index, ref in enumerate(refs[:-1]):
            refs[-1][index * rows : (index + 1) * rows, :] = ref[...]

    return pl.pallas_call(
        body,
        out_shape=jax.ShapeDtypeStruct((rows * len(parts), cols), parts[0].dtype),
        in_specs=[vmem] * len(parts),
        out_specs=vmem,
        name="join",
        **params(moved=1 << 20),
    )(*parts)


def attend_body(offsets, is_first, is_last, info_ref, low_ref, q_ref, *refs):
    count = len(offsets)
    k_refs, v_refs, refs = refs[:count], refs[count : 2 * count], refs[2 * count :]
    if is_first:
        (k1_ref, v1_ref), refs = refs[:2], refs[2:]
    else:
        (sum_in, max_in), refs = refs[:2], refs[2:]
    if is_last:
        (out_ref, sum_out, max_out), refs = (refs[0], sum_in, max_in), refs[1:]
    else:
        (sum_out, max_out), refs = refs[:2], refs[2:]
    keys, values, bias = refs
    z0, y_hi, first = info_ref[0], info_ref[1], info_ref[2]
    low_first, low_last = info_ref[3], info_ref[4]
    rows = low_ref.shape[0]
    head = pl.program_id(0)
    total_rows = q_ref.shape[1]
    width = count * PAIR
    to_two = math.log2(math.e) / math.sqrt(HD)

    needed, whole, starts = False, True, []
    for off in offsets:
        z = (z0 + off + 8) % 8
        start = z * PAIR
        starts.append(start)
        needed = needed | ((z <= z0) & (start + PAIR - 1 >= low_first))
        whole = whole & (z < z0) & (start >= low_last)

    for index in range(count):
        at = slice(index * PAIR, (index + 1) * PAIR)
        keys[at, :] = k_refs[index][...]
        values[at, :HD] = v_refs[index][...]
    values[:, HD:] = jnp.ones((width, HD), jnp.bfloat16)

    def tile(at, biased):
        scores = lax.dot_general(
            q_ref[head, at, :], keys[...], (((1,), (1,)), ((), ())), preferred_element_type=jnp.float32
        )
        if biased:
            scores = (scores.reshape(TILE // rows, rows, width) + bias[...][None]).reshape(TILE, width)
        best = scores[:, :HD]
        for part in range(1, width // HD):
            best = jnp.maximum(best, scores[:, part * HD : (part + 1) * HD])
        best = jnp.broadcast_to(jnp.max(best, axis=1, keepdims=True), (TILE, HD))
        if is_first:
            index = at.start // rows
            if (index // 2) % 2 == 1:
                q = q_ref[head, at, :].astype(jnp.float32).reshape(TILE // rows, rows, HD)
                diagonal = jnp.sum(q * k1_ref[...].astype(jnp.float32)[None], axis=-1, keepdims=True)
                old = jnp.broadcast_to(diagonal, (TILE // rows, rows, HD)).reshape(TILE, HD)
                value = v1_ref[...].astype(jnp.float32)
                begin = jnp.concatenate([value] * (TILE // rows), axis=0), jnp.ones((TILE, HD), jnp.float32)
            else:
                old, begin = None, None
        else:
            old = max_in[head, at, :]
            begin = sum_in[head, at, :HD], sum_in[head, at, HD:]
        new = best if old is None else jnp.maximum(old, best)
        shifted = new * to_two
        weights = jnp.concatenate(
            [
                jnp.exp2(scores[:, part * HD : (part + 1) * HD] * to_two - shifted).astype(jnp.bfloat16)
                for part in range(width // HD)
            ],
            axis=1,
        )
        found = jnp.dot(weights, values[...], preferred_element_type=jnp.float32)
        if old is None:
            sum_out[head, at, :] = found
        else:
            factor = jnp.exp2(old * to_two - shifted)
            sum_out[head, at, :HD] = begin[0] * factor + found[:, :HD]
            sum_out[head, at, HD:] = begin[1] * factor + found[:, HD:]
        max_out[head, at, :] = new

    def run(biased):
        for start in range(0, total_rows, TILE):
            tile(slice(start, start + TILE), biased)

    def set_bias():
        token = first + lax.broadcasted_iota(jnp.int32, (rows, PAIR), 0)
        lane = lax.broadcasted_iota(jnp.int32, (rows, PAIR), 1)
        inside = (lane + y_hi * (PAIR // 2)) & (PAIR - 1)
        for index, start in enumerate(starts):
            key = start + inside
            allowed = (key <= token) & (key >= low_ref[...])
            bias[:, index * PAIR : (index + 1) * PAIR] = jnp.where(allowed, 0.0, NEG)

    if is_first:
        set_bias()
        run(True)
    else:

        @pl.when(whole)
        def _():
            run(False)

        @pl.when(needed & jnp.logical_not(whole))
        def _():
            set_bias()
            run(True)

    if is_last:
        for index in range(total_rows // rows):
            source, step, half = index // 4, (index // 2) % 2, index % 2
            at = slice(index * rows, (index + 1) * rows)
            column = (source * 2 + half) * HD
            result = sum_out[head, at, :HD] / sum_out[head, at, HD:]
            out_ref[step, :, column : column + HD] = result.astype(jnp.bfloat16)


def attend(info, low, rotated, pieces, kv1=None, state=None, is_last=False):
    is_first = state is None
    offsets = tuple(off for off, _ in pieces)
    blocks = [block for _, block in pieces]
    count = len(blocks)
    total_rows = rotated.shape[1]
    rows = low.shape[0]
    whole = lambda h: (0, 0)
    key_col = lambda h: (0, h)
    value_col = lambda h: (0, KVH + h)
    sums = pltpu.VMEM((KVH, total_rows, 2 * HD), jnp.float32)
    maxima = pltpu.VMEM((KVH, total_rows, HD), jnp.float32)
    state_specs = [pl.BlockSpec(memory_space=pltpu.VMEM)] * 2
    in_specs = [
        pl.BlockSpec(memory_space=pltpu.SMEM),
        pl.BlockSpec((rows, 1), whole),
        pl.BlockSpec(memory_space=pltpu.VMEM),
    ]
    in_specs += [pl.BlockSpec((PAIR, HD), key_col)] * count + [pl.BlockSpec((PAIR, HD), value_col)] * count
    scratch = [
        pltpu.VMEM((count * PAIR, HD), jnp.bfloat16),
        pltpu.VMEM((count * PAIR, 2 * HD), jnp.bfloat16),
        pltpu.VMEM((rows, count * PAIR), jnp.float32),
    ]
    operands = [info, low, rotated, *blocks, *blocks]
    if is_first:
        in_specs += [pl.BlockSpec((rows, HD), key_col), pl.BlockSpec((rows, HD), value_col)]
        operands += [kv1, kv1]
    else:
        in_specs += state_specs
        operands += list(state)
    if is_last:
        out_shape = jax.ShapeDtypeStruct((2, rows, QH * HD), jnp.bfloat16)
        out_specs = pl.BlockSpec((2, rows, 8 * HD), lambda h: (0, 0, h))
        aliases = {}
    else:
        out_shape, out_specs = (sums, maxima), tuple(state_specs)
        aliases = {} if is_first else {len(operands) - 2: 0, len(operands) - 1: 1}
    return pl.pallas_call(
        functools.partial(attend_body, offsets, is_first, is_last),
        out_shape=out_shape,
        grid=(KVH,),
        in_specs=in_specs,
        out_specs=out_specs,
        scratch_shapes=scratch,
        input_output_aliases=aliases,
        name="attend_first" if is_first else "attend_last" if is_last else "attend_next",
        **params(
            flops=4 * KVH * total_rows * count * PAIR * 2 * HD,
            moved=24 << 20,
            exps=KVH * total_rows * count * PAIR,
            vmem=VMEM_ATTEND,
        ),
    )(*operands)


def on_device(hidden, norm_gain, kv_weight, queries, positions):
    steps, rows, width = hidden.shape
    grp, tp = lax.axis_index("grp"), lax.axis_index("tp")
    x, y, z, core = coords(grp, tp)
    where = jnp.stack([x, y, z, core]).astype(jnp.int32)

    up, down = shift(kv_weight, dz=1), shift(kv_weight, dz=-1)
    found = [kv_weight, up, down]
    queries, _, _ = lax.optimization_barrier((queries, up, down))
    keep, low, high = split(where, queries, rows)
    low, high = shift(low, dy=1), shift(high, dy=-1)
    for step in (2, 3):
        up, down = shift(up, dz=1), shift(down, dz=-1)
        found += [up, down]
    up, down, low, high = lax.optimization_barrier((up, down, low, high))
    low, high = shift(low, dy=1), shift(high, dy=-1)
    found.append(shift(up, dz=1))
    along_a, along_b = arrange(where, found)
    sent, _ = lax.optimization_barrier((jnp.stack([keep, jnp.concatenate([low, high])], axis=1), along_a))
    local_queries = lax.all_to_all(
        sent,
        "tp",
        split_axis=0,
        concat_axis=0,
        axis_index_groups=[list(range(0, 16, 2)), list(range(1, 16, 2))],
        tiled=True,
    )
    up_a, down_a = both_ways(along_a, along_a, "dy")
    up_b, down_b = both_ways(along_b, along_b, "dx")

    x_up, x_down, y_up, y_down = pack(
        "pack_low",
        (along_a, up_a, down_a, along_b, up_b, down_b),
        ((4, 0, H_B), (0, 0, N_A), (1, 0, N_A)),
        ((5, H_B, N_B), (0, 0, N_A), (1, 0, N_A)),
        ((1, 0, H_A), (3, 0, N_B), (4, 0, N_B)),
        ((2, H_A, N_A), (3, 0, N_B), (4, 0, N_B)),
    )
    hidden, _ = lax.optimization_barrier((hidden, x_up))
    mine, other = norm(hidden.reshape(steps * rows, width), norm_gain[None, :], where[3:])
    up2_x, down2_x = both_ways(x_up, x_down, "dx")
    up2_y, down2_y = both_ways(y_up, y_down, "dy")
    up2_x, down2_x, up2_y, down2_y, mine, other = lax.optimization_barrier(
        (up2_x, down2_x, up2_y, down2_y, mine, other)
    )
    other = shift(other, swap=True)

    x_up, x_down, y_up, y_down = pack(
        "pack_high",
        (down_a, down_b, up2_x, down2_x, up2_y, down2_y),
        ((0, 0, N_A), (4, 0, H_A), (5, 0, H_A), (2, H_B, H_B + N_A)),
        ((0, 0, N_A), (4, 0, H_A), (5, 0, H_A), (3, H_B + N_A, H_B + 2 * N_A)),
        ((1, 0, N_B), (2, 0, H_B), (3, 0, H_B), (4, H_A, H_A + N_B)),
        ((1, 0, N_B), (2, 0, H_B), (3, 0, H_B), (5, H_A + N_B, H_A + 2 * N_B)),
    )
    up3_x, down3_x = both_ways(x_up, x_down, "dx")
    up3_y, down3_y = both_ways(y_up, y_down, "dy")

    x_up, x_down, y_up, y_down = pack(
        "pack_far",
        (up3_x, down3_x, up3_y, down3_y),
        ((0, 0, N_A),),
        ((1, N_A, 2 * N_A),),
        ((2, 0, N_B),),
        ((3, N_B, 2 * N_B),),
    )
    up4_x, down4_x = both_ways(x_up, x_down, "dx")
    up4_y, down4_y = both_ways(y_up, y_down, "dy")

    freqs = rope_base ** (-jnp.arange(HD // 2, dtype=jnp.float32) * 2.0 / HD)
    angles = positions.astype(jnp.float32)[:, None] * freqs[None, :]
    cosine, sine = jnp.cos(angles), jnp.sin(angles)
    cosine = jnp.concatenate([cosine, cosine], axis=-1)
    sine = jnp.concatenate([-sine, sine], axis=-1)

    near = (along_a, up_a, down_a, up2_x, down2_x, up3_x, down3_x, up2_y, down2_y, up3_y, down3_y)
    parts = project(project_near_body, "project_near", 3, where, mine, other, near)
    far = (along_b, up_b, down_b, up2_x, down2_x, up3_x, down3_x, up4_x, down4_x, up3_y, down3_y, up4_y, down4_y)
    own, sent_part = project(project_far_body, "project_far", 1, where, mine, other, far, parts)
    got = shift(sent_part, swap=True)
    low_half, high_half, kv1 = keys_values(own, got, cosine, sine)

    first_up = shift(low_half, dy=1)
    first_down = shift(high_half, dy=-1)
    local_queries, _ = lax.optimization_barrier((local_queries, low_half))
    rotated = rotate(where, local_queries, cosine, sine)
    pair = join(low_half, high_half, shift(first_up, dy=1), shift(first_down, dy=-1))

    first = (tp * rows).astype(jnp.int32)
    low = first + jnp.arange(rows, dtype=jnp.int32) - positions
    info = jnp.stack([z.astype(jnp.int32), (tp % 2).astype(jnp.int32), first, low[0], low[rows - 1]])
    low = low[:, None]

    up, down = pair, pair
    state = attend(info, low, rotated, [(0, pair)], kv1=kv1)
    for step in (1, 2, 3):
        up, down = shift(up, dz=1), shift(down, dz=-1)
        up, down, *state = lax.optimization_barrier((up, down, *state))
        if step == 3:
            last = shift(up[: PAIR // 2], dz=1), shift(down[PAIR // 2 :], dz=-1)
        state = attend(info, low, rotated, [(-step, up), (step, down)], state=state)
    return attend(info, low, rotated, [(-4, jnp.concatenate(last))], state=state, is_last=True)


def solution(mesh):
    placed = (
        P(None, ("grp", "tp"), None),
        P(),
        P(("grp", "tp"), None),
        P(None, "grp", "tp"),
        P(("grp", "tp")),
    )
    return jax.shard_map(
        on_device,
        mesh=mesh,
        in_specs=placed,
        out_specs=P(None, ("grp", "tp"), None),
        check_vma=False,
    )
```

```python
import functools
import math

import jax
import jax.numpy as jnp
from jax import lax
from jax.experimental import pallas as pl
from jax.experimental.pallas import tpu as pltpu
from jax.sharding import PartitionSpec as P

HD = 128
QH = 32
KVH = 4
BOTH = ("grp", "tp")
COLS_A = 512
COLS_B = 512
N_A, N_B = COLS_A // 128 * 8, COLS_B // 128 * 8
H_A, H_B = N_A // 2, N_B // 2
PAIR = 256
TILE = 256
VMEM = 12 * 1024 * 1024
VMEM_PROJECT = 24 * 1024 * 1024
VMEM_ATTEND = 16 * 1024 * 1024
NEG = -1e30
rope_base = 500000.0


def coords(grp, tp):
    return grp // 4, (tp % 2) * 2 + (grp // 2) % 2, tp // 2, grp % 2


def place(x, y, z, core):
    return ((x * 2 + y % 2) * 2 + core) * 16 + z * 2 + y // 2


def shift(value, dx=0, dy=0, dz=0, swap=False):
    pairs = []
    for device in range(256):
        x, y, z, core = coords(device // 16, device % 16)
        target = place((x + dx) % 4, (y + dy) % 4, (z + dz) % 8, 1 - core if swap else core)
        pairs.append((device, target))
    return lax.ppermute(value, BOTH, pairs)


def params(flops=0, moved=0, exps=0, vmem=VMEM):
    return dict(
        compiler_params=pltpu.CompilerParams(vmem_limit_bytes=vmem),
        cost_estimate=pl.CostEstimate(flops=flops, bytes_accessed=moved, transcendentals=exps),
    )


def arrange_body(where_ref, *refs):
    a_ref, b_ref = refs[8:]
    z0 = where_ref[2]
    for off, ref in zip((0, -1, 1, -2, 2, -3, 3, -4), refs[:8]):
        z = (z0 + off + 8) % 8
        for part in range(8):
            block = ref[:, part * 128 : (part + 1) * 128]
            if part * 128 < COLS_A:
                a_ref[part * 8 + z] = block
            else:
                b_ref[part * 8 - N_A + z] = block


def blocks_of(count):
    return jax.ShapeDtypeStruct((count, 32, 128), jnp.bfloat16)


def arrange(where, pieces):
    vmem = pl.BlockSpec(memory_space=pltpu.VMEM)
    return pl.pallas_call(
        arrange_body,
        out_shape=(blocks_of(N_A), blocks_of(N_B)),
        in_specs=[pl.BlockSpec(memory_space=pltpu.SMEM)] + [vmem] * 8,
        out_specs=(vmem, vmem),
        name="arrange",
        **params(moved=1 << 20),
    )(where, *pieces)


def pack(name, arrays, *plans):
    vmem = pl.BlockSpec(memory_space=pltpu.VMEM)

    def body(*refs):
        for plan, out_ref in zip(plans, refs[len(arrays) :]):
            at = 0
            for number, begin, end in plan:
                out_ref[at : at + end - begin] = refs[number][begin:end]
                at += end - begin

    return pl.pallas_call(
        body,
        out_shape=tuple(blocks_of(sum(end - begin for _, begin, end in plan)) for plan in plans),
        in_specs=[vmem] * len(arrays),
        out_specs=(vmem,) * len(plans),
        name=name,
        **params(moved=4 << 20),
    )(*arrays)


def both_ways(up, down, axis):
    return shift(up, **{axis: 1}), shift(down, **{axis: -1})


def norm_body(core_ref, hidden_ref, gain_ref, mine_ref, other_ref):
    core = core_ref[0]
    wide = hidden_ref[...].astype(jnp.float32)
    scale = lax.rsqrt(jnp.mean(wide * wide, axis=-1, keepdims=True) + 1e-05)
    for group in range(8):
        for out_ref, which in ((mine_ref, core), (other_ref, 1 - core)):
            start = pl.multiple_of((2 * group + which) * 512, 512)
            part = hidden_ref[:, pl.ds(start, 512)].astype(jnp.float32)
            gain = gain_ref[:, pl.ds(start, 512)]
            out_ref[:, group * 512 : (group + 1) * 512] = (part * scale * gain).astype(jnp.bfloat16)


def norm(hidden, gain, core):
    rows, width = hidden.shape
    out = jax.ShapeDtypeStruct((rows, width // 2), jnp.bfloat16)
    return pl.pallas_call(
        norm_body,
        out_shape=(out, out),
        grid=(rows // 64,),
        in_specs=[
            pl.BlockSpec(memory_space=pltpu.SMEM),
            pl.BlockSpec((64, width), lambda i: (i, 0)),
            pl.BlockSpec((1, width), lambda i: (0, 0)),
        ],
        out_specs=(
            pl.BlockSpec((64, width // 2), lambda i: (i, 0)),
            pl.BlockSpec((64, width // 2), lambda i: (i, 0)),
        ),
        compiler_params=pltpu.CompilerParams(vmem_limit_bytes=VMEM),
        name="norm",
    )(core, hidden, gain)


def segments(count, pieces):
    at = 0
    for ref, begin, blocks in pieces:
        while blocks:
            run = min(blocks, 8 - at % 8)
            yield ref, begin, at // 8 * 128, at % 8, run
            at, begin, blocks = at + run, begin + run, blocks - run
    assert at == count


class Puts:
    def __init__(self, where_ref, sems, weight_a, weight_b):
        self.x, self.y, self.sems, self.weight_a, self.weight_b = where_ref[0], where_ref[1], sems, weight_a, weight_b
        self.copies = []

    def start(self, source, target):
        copy = pltpu.make_async_copy(source, target, self.sems.at[len(self.copies)])
        copy.start()
        self.copies.append(copy)

    def wait(self, begin, end):
        for copy in self.copies[begin:end]:
            copy.wait()

    def a(self, slot, off_y, *pieces):
        y = (self.y + off_y + 4) % 4
        for ref, begin, col, z, run in segments(N_A, pieces):
            target = self.weight_a.at[slot, y % 2, pl.ds(z, run), y // 2, :, pl.ds(col, 128)]
            self.start(ref.at[pl.ds(begin, run)], target)

    def b(self, off_x, off_y, *pieces):
        x, y = (self.x + off_x + 4) % 4, (self.y + off_y + 4) % 4
        for ref, begin, col, z, run in segments(N_B, pieces):
            target = self.weight_b.at[x, pl.ds(z, run), y // 2, :, pl.ds(col, 128)]
            self.start(ref.at[pl.ds(begin, run)], target)


def times_a(where_ref, rows_ref, weight, offsets):
    total = None
    for slot, off in enumerate(offsets):
        x = (where_ref[0] + off + 4) % 4
        lhs = rows_ref[:, pl.ds(pl.multiple_of(x * 1024, 1024), 1024)]
        part = jnp.dot(lhs, weight[slot].reshape(1024, COLS_A), preferred_element_type=jnp.float32)
        total = part if total is None else total + part
    return total


def times_b(where_ref, rows_ref, weight, low):
    total = None
    for x in range(4):
        lhs = rows_ref[:, pl.ds(pl.multiple_of((x * 2 + low) * 512, 512), 512)]
        part = jnp.dot(lhs, weight[x].reshape(512, weight.shape[-1]), preferred_element_type=jnp.float32)
        total = part if total is None else total + part
    return total


def project_near_body(where_ref, mine_ref, other_ref, *refs):
    own_a, up_a, down_a, up2_x, down2_x, up3_x, down3_x, up2_y, down2_y, up3_y, down3_y = refs[:11]
    mine_out, other_out, weight_a, weight_b, sems = refs[11:]
    puts = Puts(where_ref, sems, weight_a, weight_b)
    puts.a(0, 0, (own_a, 0, N_A))
    puts.a(0, -1, (up_a, 0, N_A))
    puts.a(0, 1, (down_a, 0, N_A))
    puts.a(0, -2, (up2_y, 0, H_A), (down2_y, 0, H_A))
    for slot, second, third in ((1, up2_x, up3_x), (2, down2_x, down3_x)):
        puts.a(slot, 0, (second, H_B, N_A))
        puts.a(slot, -1, (second, H_B + N_A, N_A))
        puts.a(slot, 1, (third, 0, N_A))
        puts.a(slot, -2, (third, N_A, N_A))
    half = len(puts.copies)
    for off, second, third in ((-1, up2_y, up3_y), (1, down2_y, down3_y)):
        puts.b(0, off, (second, H_A, N_B))
        puts.b(-1, off, (second, H_A + N_B, N_B))
        puts.b(1, off, (third, 0, N_B))
        puts.b(-2, off, (third, N_B, N_B))
    low = 1 - where_ref[1] % 2
    puts.wait(0, half)
    for rows_ref, out_ref in ((mine_ref, mine_out), (other_ref, other_out)):
        out_ref[:, :COLS_A] = times_a(where_ref, rows_ref, weight_a, (0, -1, 1))
    puts.wait(half, None)
    for rows_ref, out_ref in ((mine_ref, mine_out), (other_ref, other_out)):
        out_ref[:, COLS_A:] = times_b(where_ref, rows_ref, weight_b, low)


def project_far_body(where_ref, mine_ref, other_ref, *refs):
    own_b, up_b, down_b, up2_x, down2_x, up3_x, down3_x, up4_x, down4_x, up3_y, down3_y, up4_y, down4_y = refs[:13]
    mine_part, other_part, mine_out, other_out, weight_a, weight_b, sems = refs[13:]
    puts = Puts(where_ref, sems, weight_a, weight_b)
    puts.a(0, 0, (up3_x, 2 * N_A, N_A))
    puts.a(0, -1, (down3_x, 2 * N_A, N_A))
    puts.a(0, 1, (up4_x, 0, N_A))
    puts.a(0, -2, (down4_x, 0, N_A))
    half = len(puts.copies)
    puts.b(0, 0, (own_b, 0, N_B))
    puts.b(-1, 0, (up_b, 0, N_B))
    puts.b(1, 0, (down_b, 0, N_B))
    puts.b(-2, 0, (up2_x, 0, H_B), (down2_x, 0, H_B))
    puts.b(0, -2, (up3_y, 2 * N_B, N_B))
    puts.b(-1, -2, (down3_y, 2 * N_B, N_B))
    puts.b(1, -2, (up4_y, 0, N_B))
    puts.b(-2, -2, (down4_y, 0, N_B))
    low = where_ref[1] % 2
    both = ((other_ref, other_part, other_out), (mine_ref, mine_part, mine_out))
    puts.wait(0, half)
    for rows_ref, part_ref, out_ref in both:
        out_ref[:, :COLS_A] = part_ref[:, :COLS_A] + times_a(where_ref, rows_ref, weight_a, (-2,))
    puts.wait(half, None)
    for rows_ref, part_ref, out_ref in both:
        out_ref[:, COLS_A:] = part_ref[:, COLS_A:] + times_b(where_ref, rows_ref, weight_b, low)


def project(body, name, slots, where, mine, other, pieces, parts=()):
    rows = mine.shape[0]
    out = pltpu.VMEM((rows, COLS_A + COLS_B), jnp.float32)
    vmem = pl.BlockSpec(memory_space=pltpu.VMEM)
    hbm = pl.BlockSpec(memory_space=pl.ANY)
    return pl.pallas_call(
        body,
        out_shape=(out, out if not parts else jax.ShapeDtypeStruct(out.shape, out.dtype)),
        in_specs=[pl.BlockSpec(memory_space=pltpu.SMEM)] + [vmem] * 2 + [hbm] * len(pieces) + [vmem] * len(parts),
        out_specs=(vmem, vmem),
        scratch_shapes=[
            pltpu.VMEM((slots, 2, 8, 2, 32, COLS_A), jnp.bfloat16),
            pltpu.VMEM((4, 8, 2, 32, COLS_B), jnp.bfloat16),
            pltpu.SemaphoreType.DMA((128,)),
        ],
        name=name,
        **params(flops=1 << 31, moved=12 << 20, vmem=VMEM_PROJECT),
    )(where, mine, other, *pieces, *parts)


def turn(values, cosine, sine):
    return values * cosine + pltpu.roll(values, 64, 1) * sine


def split_body(where_ref, q_ref, keep_ref, low_ref, high_ref):
    y_hi, z = where_ref[1] // 2, pl.program_id(0)
    keep_ref[0] = q_ref[:, 0, y_hi]

    @pl.when(z < 4)
    def _():
        low_ref[0] = q_ref[:, 0, 1 - y_hi]

    @pl.when(z >= 4)
    def _():
        high_ref[0] = q_ref[:, 0, 1 - y_hi]


def split(where, queries, rows):
    steps = queries.shape[0]
    shape = (steps, rows, 2 * HD)
    block = (1, *shape)
    return pl.pallas_call(
        split_body,
        out_shape=tuple(jax.ShapeDtypeStruct((count, *shape), jnp.bfloat16) for count in (8, 4, 4)),
        grid=(8,),
        in_specs=[
            pl.BlockSpec(memory_space=pltpu.SMEM),
            pl.BlockSpec((steps, 1, 2, rows, 2 * HD), lambda z: (0, z, 0, 0, 0)),
        ],
        out_specs=(
            pl.BlockSpec(block, lambda z: (z, 0, 0, 0)),
            pl.BlockSpec(block, lambda z: (jnp.minimum(z, 3), 0, 0, 0)),
            pl.BlockSpec(block, lambda z: (jnp.maximum(z, 4) - 4, 0, 0, 0)),
        ),
        name="split",
        **params(moved=4 << 20),
    )(where, queries.reshape(steps, 8, 2, rows, 2 * HD))


def rotate_body(where_ref, q_ref, cos_ref, sin_ref, out_ref):
    rows = cos_ref.shape[0]
    cosine, sine = cos_ref[...], sin_ref[...]
    y_hi, head = where_ref[1] // 2, pl.program_id(0)
    for low_z in range(2):
        for other in range(2):
            source = 2 * low_z + (y_hi if other == 0 else 1 - y_hi)
            for step in range(2):
                for half in range(2):
                    at = pl.multiple_of((source * 4 + step * 2 + half) * rows, rows)
                    value = q_ref[low_z, other, step, :, half * HD : (half + 1) * HD].astype(jnp.float32)
                    out_ref[head, pl.ds(at, rows), :] = turn(value, cosine, sine).astype(jnp.bfloat16)


def rotate(where, queries, cosine, sine):
    rows = cosine.shape[0]
    whole = lambda h: (0, 0)
    return pl.pallas_call(
        rotate_body,
        out_shape=pltpu.VMEM((KVH, 16 * rows, HD), jnp.bfloat16),
        grid=(KVH,),
        in_specs=[
            pl.BlockSpec(memory_space=pltpu.SMEM),
            pl.BlockSpec((2, 2, 2, rows, 2 * HD), lambda h: (h, 0, 0, 0, 0)),
            pl.BlockSpec((rows, HD), whole),
            pl.BlockSpec((rows, HD), whole),
        ],
        out_specs=pl.BlockSpec(memory_space=pltpu.VMEM),
        name="rotate",
        **params(flops=1 << 23, moved=4 << 20),
    )(where, queries, cosine, sine)


def keys_values_body(own_ref, got_ref, cos_ref, sin_ref, low_ref, high_ref, second_ref):
    rows = second_ref.shape[0]
    cosine, sine = cos_ref[...], sin_ref[...]
    for step in range(2):
        for head in range(2 * KVH):
            cols = slice(head * HD, (head + 1) * HD)
            part = own_ref[step * rows : (step + 1) * rows, cols]
            part = part + got_ref[step * rows : (step + 1) * rows, cols]
            if head < KVH:
                part = turn(part, cosine, sine)
            part = part.astype(jnp.bfloat16)
            if step == 0:
                low_ref[:, cols] = part[: rows // 2]
                high_ref[:, cols] = part[rows // 2 :]
            else:
                second_ref[:, cols] = part


def keys_values(own, got, cosine, sine):
    rows, cols = own.shape
    half = jax.ShapeDtypeStruct((rows // 4, cols), jnp.bfloat16)
    vmem = pl.BlockSpec(memory_space=pltpu.VMEM)
    return pl.pallas_call(
        keys_values_body,
        out_shape=(half, half, jax.ShapeDtypeStruct((rows // 2, cols), jnp.bfloat16)),
        in_specs=[vmem] * 4,
        out_specs=(vmem, vmem, vmem),
        name="keys_values",
        **params(flops=1 << 20, moved=4 << 20),
    )(own, got, cosine, sine)


def join(*parts):
    rows, cols = parts[0].shape
    vmem = pl.BlockSpec(memory_space=pltpu.VMEM)

    def body(*refs):
        for index, ref in enumerate(refs[:-1]):
            refs[-1][index * rows : (index + 1) * rows, :] = ref[...]

    return pl.pallas_call(
        body,
        out_shape=jax.ShapeDtypeStruct((rows * len(parts), cols), parts[0].dtype),
        in_specs=[vmem] * len(parts),
        out_specs=vmem,
        name="join",
        **params(moved=1 << 20),
    )(*parts)


def attend_body(offsets, is_first, is_last, info_ref, low_ref, q_ref, *refs):
    count = len(offsets)
    k_refs, v_refs, refs = refs[:count], refs[count : 2 * count], refs[2 * count :]
    if is_first:
        (k1_ref, v1_ref), refs = refs[:2], refs[2:]
    else:
        (sum_in, max_in), refs = refs[:2], refs[2:]
    if is_last:
        (out_ref, sum_out, max_out), refs = (refs[0], sum_in, max_in), refs[1:]
    else:
        (sum_out, max_out), refs = refs[:2], refs[2:]
    keys, values, bias = refs
    z0, y_hi, first = info_ref[0], info_ref[1], info_ref[2]
    low_first, low_last = info_ref[3], info_ref[4]
    rows = low_ref.shape[0]
    head = pl.program_id(0)
    total_rows = q_ref.shape[1]
    width = count * PAIR
    to_two = math.log2(math.e) / math.sqrt(HD)

    needed, whole, starts = False, True, []
    for off in offsets:
        z = (z0 + off + 8) % 8
        start = z * PAIR
        starts.append(start)
        needed = needed | ((z <= z0) & (start + PAIR - 1 >= low_first))
        whole = whole & (z < z0) & (start >= low_last)

    for index in range(count):
        at = slice(index * PAIR, (index + 1) * PAIR)
        keys[at, :] = k_refs[index][...]
        values[at, :HD] = v_refs[index][...]
    values[:, HD:] = jnp.ones((width, HD), jnp.bfloat16)

    def tile(at, biased):
        scores = lax.dot_general(
            q_ref[head, at, :], keys[...], (((1,), (1,)), ((), ())), preferred_element_type=jnp.float32
        )
        if biased:
            scores = (scores.reshape(TILE // rows, rows, width) + bias[...][None]).reshape(TILE, width)
        best = scores[:, :HD]
        for part in range(1, width // HD):
            best = jnp.maximum(best, scores[:, part * HD : (part + 1) * HD])
        best = jnp.broadcast_to(jnp.max(best, axis=1, keepdims=True), (TILE, HD))
        if is_first:
            index = at.start // rows
            if (index // 2) % 2 == 1:
                q = q_ref[head, at, :].astype(jnp.float32).reshape(TILE // rows, rows, HD)
                diagonal = jnp.sum(q * k1_ref[...].astype(jnp.float32)[None], axis=-1, keepdims=True)
                old = jnp.broadcast_to(diagonal, (TILE // rows, rows, HD)).reshape(TILE, HD)
                value = v1_ref[...].astype(jnp.float32)
                begin = jnp.concatenate([value] * (TILE // rows), axis=0), jnp.ones((TILE, HD), jnp.float32)
            else:
                old, begin = None, None
        else:
            old = max_in[head, at, :]
            begin = sum_in[head, at, :HD], sum_in[head, at, HD:]
        new = best if old is None else jnp.maximum(old, best)
        shifted = new * to_two
        weights = jnp.concatenate(
            [
                jnp.exp2(scores[:, part * HD : (part + 1) * HD] * to_two - shifted).astype(jnp.bfloat16)
                for part in range(width // HD)
            ],
            axis=1,
        )
        found = jnp.dot(weights, values[...], preferred_element_type=jnp.float32)
        if old is None:
            sum_out[head, at, :] = found
        else:
            factor = jnp.exp2(old * to_two - shifted)
            sum_out[head, at, :HD] = begin[0] * factor + found[:, :HD]
            sum_out[head, at, HD:] = begin[1] * factor + found[:, HD:]
        max_out[head, at, :] = new

    def run(biased):
        for start in range(0, total_rows, TILE):
            tile(slice(start, start + TILE), biased)

    def set_bias():
        token = first + lax.broadcasted_iota(jnp.int32, (rows, PAIR), 0)
        lane = lax.broadcasted_iota(jnp.int32, (rows, PAIR), 1)
        inside = (lane + y_hi * (PAIR // 2)) & (PAIR - 1)
        for index, start in enumerate(starts):
            key = start + inside
            allowed = (key <= token) & (key >= low_ref[...])
            bias[:, index * PAIR : (index + 1) * PAIR] = jnp.where(allowed, 0.0, NEG)

    if is_first:
        set_bias()
        run(True)
    else:

        @pl.when(whole)
        def _():
            run(False)

        @pl.when(needed & jnp.logical_not(whole))
        def _():
            set_bias()
            run(True)

    if is_last:
        for index in range(total_rows // rows):
            source, step, half = index // 4, (index // 2) % 2, index % 2
            at = slice(index * rows, (index + 1) * rows)
            column = (source * 2 + half) * HD
            result = sum_out[head, at, :HD] / sum_out[head, at, HD:]
            out_ref[step, :, column : column + HD] = result.astype(jnp.bfloat16)


def attend(info, low, rotated, pieces, kv1=None, state=None, is_last=False):
    is_first = state is None
    offsets = tuple(off for off, _ in pieces)
    blocks = [block for _, block in pieces]
    count = len(blocks)
    total_rows = rotated.shape[1]
    rows = low.shape[0]
    whole = lambda h: (0, 0)
    key_col = lambda h: (0, h)
    value_col = lambda h: (0, KVH + h)
    sums = pltpu.VMEM((KVH, total_rows, 2 * HD), jnp.float32)
    maxima = pltpu.VMEM((KVH, total_rows, HD), jnp.float32)
    state_specs = [pl.BlockSpec(memory_space=pltpu.VMEM)] * 2
    in_specs = [
        pl.BlockSpec(memory_space=pltpu.SMEM),
        pl.BlockSpec((rows, 1), whole),
        pl.BlockSpec(memory_space=pltpu.VMEM),
    ]
    in_specs += [pl.BlockSpec((PAIR, HD), key_col)] * count + [pl.BlockSpec((PAIR, HD), value_col)] * count
    scratch = [
        pltpu.VMEM((count * PAIR, HD), jnp.bfloat16),
        pltpu.VMEM((count * PAIR, 2 * HD), jnp.bfloat16),
        pltpu.VMEM((rows, count * PAIR), jnp.float32),
    ]
    operands = [info, low, rotated, *blocks, *blocks]
    if is_first:
        in_specs += [pl.BlockSpec((rows, HD), key_col), pl.BlockSpec((rows, HD), value_col)]
        operands += [kv1, kv1]
    else:
        in_specs += state_specs
        operands += list(state)
    if is_last:
        out_shape = jax.ShapeDtypeStruct((2, rows, QH * HD), jnp.bfloat16)
        out_specs = pl.BlockSpec((2, rows, 8 * HD), lambda h: (0, 0, h))
        aliases = {}
    else:
        out_shape, out_specs = (sums, maxima), tuple(state_specs)
        aliases = {} if is_first else {len(operands) - 2: 0, len(operands) - 1: 1}
    return pl.pallas_call(
        functools.partial(attend_body, offsets, is_first, is_last),
        out_shape=out_shape,
        grid=(KVH,),
        in_specs=in_specs,
        out_specs=out_specs,
        scratch_shapes=scratch,
        input_output_aliases=aliases,
        name="attend_first" if is_first else "attend_last" if is_last else "attend_next",
        **params(
            flops=4 * KVH * total_rows * count * PAIR * 2 * HD,
            moved=24 << 20,
            exps=KVH * total_rows * count * PAIR,
            vmem=VMEM_ATTEND,
        ),
    )(*operands)


def on_device(hidden, norm_gain, kv_weight, queries, positions):
    steps, rows, width = hidden.shape
    grp, tp = lax.axis_index("grp"), lax.axis_index("tp")
    x, y, z, core = coords(grp, tp)
    where = jnp.stack([x, y, z, core]).astype(jnp.int32)

    up, down = shift(kv_weight, dz=1), shift(kv_weight, dz=-1)
    found = [kv_weight, up, down]
    queries, _, _ = lax.optimization_barrier((queries, up, down))
    keep, low, high = split(where, queries, rows)
    low, high = shift(low, dy=1), shift(high, dy=-1)
    for step in (2, 3):
        up, down = shift(up, dz=1), shift(down, dz=-1)
        found += [up, down]
    up, down, low, high = lax.optimization_barrier((up, down, low, high))
    low, high = shift(low, dy=1), shift(high, dy=-1)
    found.append(shift(up, dz=1))
    along_a, along_b = arrange(where, found)
    up_a, down_a = both_ways(along_a, along_a, "dy")
    up_b, down_b = both_ways(along_b, along_b, "dx")

    x_up, x_down, y_up, y_down = pack(
        "pack_low",
        (along_a, up_a, down_a, along_b, up_b, down_b),
        ((4, 0, H_B), (0, 0, N_A), (1, 0, N_A)),
        ((5, H_B, N_B), (0, 0, N_A), (1, 0, N_A)),
        ((1, 0, H_A), (3, 0, N_B), (4, 0, N_B)),
        ((2, H_A, N_A), (3, 0, N_B), (4, 0, N_B)),
    )
    hidden, _ = lax.optimization_barrier((hidden, x_up))
    mine, other = norm(hidden.reshape(steps * rows, width), norm_gain[None, :], where[3:])
    up2_x, down2_x = both_ways(x_up, x_down, "dx")
    up2_y, down2_y = both_ways(y_up, y_down, "dy")
    up2_x, down2_x, up2_y, down2_y, mine, other = lax.optimization_barrier(
        (up2_x, down2_x, up2_y, down2_y, mine, other)
    )
    other = shift(other, swap=True)

    x_up, x_down, y_up, y_down = pack(
        "pack_high",
        (down_a, down_b, up2_x, down2_x, up2_y, down2_y),
        ((0, 0, N_A), (4, 0, H_A), (5, 0, H_A), (2, H_B, H_B + N_A)),
        ((0, 0, N_A), (4, 0, H_A), (5, 0, H_A), (3, H_B + N_A, H_B + 2 * N_A)),
        ((1, 0, N_B), (2, 0, H_B), (3, 0, H_B), (4, H_A, H_A + N_B)),
        ((1, 0, N_B), (2, 0, H_B), (3, 0, H_B), (5, H_A + N_B, H_A + 2 * N_B)),
    )
    up3_x, down3_x = both_ways(x_up, x_down, "dx")
    up3_y, down3_y = both_ways(y_up, y_down, "dy")
    sent = jnp.stack([keep, jnp.concatenate([low, high])], axis=1)
    sent, _ = lax.optimization_barrier((sent, up3_y))
    local_queries = lax.all_to_all(
        sent,
        "tp",
        split_axis=0,
        concat_axis=0,
        axis_index_groups=[list(range(0, 16, 2)), list(range(1, 16, 2))],
        tiled=True,
    )

    x_up, x_down, y_up, y_down = pack(
        "pack_far",
        (up3_x, down3_x, up3_y, down3_y),
        ((0, 0, N_A),),
        ((1, N_A, 2 * N_A),),
        ((2, 0, N_B),),
        ((3, N_B, 2 * N_B),),
    )
    up4_x, down4_x = both_ways(x_up, x_down, "dx")
    up4_y, down4_y = both_ways(y_up, y_down, "dy")

    freqs = rope_base ** (-jnp.arange(HD // 2, dtype=jnp.float32) * 2.0 / HD)
    angles = positions.astype(jnp.float32)[:, None] * freqs[None, :]
    cosine, sine = jnp.cos(angles), jnp.sin(angles)
    cosine = jnp.concatenate([cosine, cosine], axis=-1)
    sine = jnp.concatenate([-sine, sine], axis=-1)

    near = (along_a, up_a, down_a, up2_x, down2_x, up3_x, down3_x, up2_y, down2_y, up3_y, down3_y)
    parts = project(project_near_body, "project_near", 3, where, mine, other, near)
    far = (along_b, up_b, down_b, up2_x, down2_x, up3_x, down3_x, up4_x, down4_x, up3_y, down3_y, up4_y, down4_y)
    own, sent_part = project(project_far_body, "project_far", 1, where, mine, other, far, parts)
    got = shift(sent_part, swap=True)
    low_half, high_half, kv1 = keys_values(own, got, cosine, sine)

    first_up = shift(low_half, dy=1)
    first_down = shift(high_half, dy=-1)
    local_queries, _ = lax.optimization_barrier((local_queries, low_half))
    rotated = rotate(where, local_queries, cosine, sine)
    pair = join(low_half, high_half, shift(first_up, dy=1), shift(first_down, dy=-1))

    first = (tp * rows).astype(jnp.int32)
    low = first + jnp.arange(rows, dtype=jnp.int32) - positions
    info = jnp.stack([z.astype(jnp.int32), (tp % 2).astype(jnp.int32), first, low[0], low[rows - 1]])
    low = low[:, None]

    up, down = pair, pair
    state = attend(info, low, rotated, [(0, pair)], kv1=kv1)
    for step in (1, 2, 3):
        up, down = shift(up, dz=1), shift(down, dz=-1)
        up, down, *state = lax.optimization_barrier((up, down, *state))
        if step == 3:
            last = shift(up[: PAIR // 2], dz=1), shift(down[PAIR // 2 :], dz=-1)
        state = attend(info, low, rotated, [(-step, up), (step, down)], state=state)
    return attend(info, low, rotated, [(-4, jnp.concatenate(last))], state=state, is_last=True)


def solution(mesh):
    placed = (
        P(None, ("grp", "tp"), None),
        P(),
        P(("grp", "tp"), None),
        P(None, "grp", "tp"),
        P(("grp", "tp")),
    )
    return jax.shard_map(
        on_device,
        mesh=mesh,
        in_specs=placed,
        out_specs=P(None, ("grp", "tp"), None),
        check_vma=False,
    )
```
